512 devices in a mesh: head: 8 (over y_hi, core), ctx: 64 (over x, y_lo, z).
Axes of the slice: x: 4, y: 8 (y_hi: 4, y_lo: 2; y = y_hi * 2 + y_lo), z: 8, core: 2. Of those that a mesh axis runs over, the one named last changes fastest.
Arguments:
- queries: bfloat16 [65536, 4096], P(('ctx', 'head')), may hold values from -8 to 8
- saved_key_rows: bfloat16 [65536, 1024], P(('ctx', 'head')), may hold values from -8 to 8
- saved_value_rows: bfloat16 [65536, 1024], P(('ctx', 'head')), may hold values from -6 to 6
- saved_output: bfloat16 [65536, 4096], P(('ctx', 'head')), may hold values from -1.5 to 1.5
- output_gradient: bfloat16 [65536, 4096], P(('ctx', 'head')), may hold values from -6 to 6
- stripe_order: int32 [64, 1024], P('ctx'), may hold values from 0 to 1023, each once within a row
Outputs:
- query_gradient: bfloat16 [65536, 4096], P(('ctx', 'head'))
- key_grad: bfloat16 [65536, 1024], P(('ctx', 'head'))
- value_grad: bfloat16 [65536, 1024], P(('ctx', 'head'))
The draws below stay inside these ranges and needn't reach their ends.
Inputs may be any that keep to these rules, and one draw needn't show every extreme that they name: Each row of stripe_order holds every number from 0 to 1023 once.
All inputs are finite; a program needn't handle non-finite values.
Results may differ from the reference program's by a relative error of at most 0.0049.
Values may be sent and summed in bfloat16 or wider, within the bound.
A program may use at most 64 MiB of HBM per device.

```python
import math
import jax
import jax.numpy as jnp
from jax import lax

QUERY_HEADS = 32
KEY_HEADS = 8
HEAD_SIZE = 128
BLOCK_TOKENS = 1024
TAIL_POSITIONS = 256
SEQUENCE_LENGTH = 65536
N_CTX = 64


def draw_queries(key, part):
    base_offset = jnp.clip(jax.random.normal(jax.random.fold_in(key, 21), (SEQUENCE_LENGTH, QUERY_HEADS * HEAD_SIZE), jnp.float32), -6.0, 6.0)
    return base_offset.astype(jnp.bfloat16)


def draw_keys(key, part):
    base_offset = jnp.clip(jax.random.normal(jax.random.fold_in(key, 31), (SEQUENCE_LENGTH, KEY_HEADS * HEAD_SIZE), jnp.float32), -6.0, 6.0)
    return base_offset


def draw_saved_key_rows(key, part):
    return draw_keys(key, part).astype(jnp.bfloat16)


def block_scale(own_key, extent, shards, smallest, high):
    def one(axis_at, parts):
        draws = jax.random.uniform(jax.random.fold_in(jax.random.fold_in(own_key, 6), axis_at), (parts,), jnp.float32, smallest / len(shards), high / len(shards))
        return jnp.repeat(jnp.exp(draws), extent[axis_at] // parts).reshape((-1,) + (1,) * (len(extent) - axis_at - 1))

    loudness = one(*shards[0])
    for cut in shards[1:]:
        loudness = loudness * one(*cut)
    return loudness


def gaussian(key, shape, deviation, reach, shards=(), held_as=jnp.bfloat16):
    values = deviation * jax.random.normal(key, shape, jnp.float32)
    if shards:
        values = values * block_scale(key, shape, shards, -0.22, 0.18)
    return jnp.clip(values, -reach, reach).astype(held_as)


def setup_inputs(seed: int = 0) -> dict:
    key_of = jax.random.split(jax.random.key(seed), 7)
    return {
        "queries": draw_queries(jax.random.fold_in(key_of[6], 71), 0),
        "saved_key_rows": draw_saved_key_rows(jax.random.fold_in(key_of[6], 71), 0),
        "saved_value_rows": gaussian(key_of[2], (SEQUENCE_LENGTH, KEY_HEADS * HEAD_SIZE), 1.0, 6.0, ((0, 512),)),
        "saved_output": gaussian(key_of[3], (SEQUENCE_LENGTH, QUERY_HEADS * HEAD_SIZE), 0.25, 1.5, ((0, 512),)),
        "output_gradient": gaussian(key_of[4], (SEQUENCE_LENGTH, QUERY_HEADS * HEAD_SIZE), 1.0, 6.0, ((0, 512),)),
        "stripe_order": jax.vmap(lambda own: jax.random.permutation(own, BLOCK_TOKENS))(jax.random.split(key_of[5], N_CTX)).reshape((N_CTX, BLOCK_TOKENS)).astype(jnp.int32),
    }


def invert_order(order_row):
    return jnp.zeros((BLOCK_TOKENS,), jnp.int32).at[order_row].set(jnp.arange(BLOCK_TOKENS, dtype=jnp.int32))

def add_rows(target, index, terms):
    return target.at[index].add(terms)

def reference(queries, saved_key_rows, saved_value_rows, saved_output, output_gradient, stripe_order):
    query_groups = QUERY_HEADS // KEY_HEADS
    score_scale = 1.0 / math.sqrt(HEAD_SIZE)
    blocked_queries = queries.reshape(N_CTX, BLOCK_TOKENS, KEY_HEADS, query_groups, HEAD_SIZE)
    gradient_blocks = output_gradient.reshape(N_CTX, BLOCK_TOKENS, KEY_HEADS, query_groups, HEAD_SIZE)
    blocked_keys = saved_key_rows.reshape(N_CTX, BLOCK_TOKENS, KEY_HEADS, HEAD_SIZE)
    blocked_values = saved_value_rows.reshape(N_CTX, BLOCK_TOKENS, KEY_HEADS, HEAD_SIZE)
    inverse = jax.vmap(invert_order)(stripe_order.astype(jnp.int32))
    tail_index = inverse[:, BLOCK_TOKENS - TAIL_POSITIONS:].astype(jnp.int32)
    key_tail = jnp.take_along_axis(blocked_keys, tail_index[:, :, None, None], axis=1)
    value_tail = jnp.take_along_axis(blocked_values, tail_index[:, :, None, None], axis=1)
    key_before = jnp.concatenate([jnp.zeros_like(key_tail[:1]), key_tail[:-1]], axis=0)
    value_before = jnp.concatenate([jnp.zeros_like(value_tail[:1]), value_tail[:-1]], axis=0)
    elementwise_products = saved_output.astype(jnp.float32) * output_gradient.astype(jnp.float32)
    delta_rows = lax.optimization_barrier(jnp.sum(elementwise_products.reshape(SEQUENCE_LENGTH, QUERY_HEADS, HEAD_SIZE), axis=2)).reshape(N_CTX, BLOCK_TOKENS, KEY_HEADS, query_groups)
    block_ids = jnp.arange(N_CTX, dtype=jnp.int32)

    def one_block(items):
        query_b, key_b, key_p, value_b, value_p, grad_b, delta_b, order_b, block_id = items
        query_f = query_b.astype(jnp.float32)
        grad_f = grad_b.astype(jnp.float32)
        keys_all = jnp.concatenate([key_b, key_p], axis=0).astype(jnp.float32)
        values_all = jnp.concatenate([value_b, value_p], axis=0).astype(jnp.float32)
        own_part = order_b[None, :] <= order_b[:, None]
        prev_part = jnp.broadcast_to(block_id > 0, (BLOCK_TOKENS, TAIL_POSITIONS))
        visible = jnp.concatenate([own_part, prev_part], axis=1)
        scores = jnp.einsum('igad,jgd->gaij', query_f, keys_all) * score_scale
        scores = jnp.where(visible, scores, -1e+30)
        row_top = lax.optimization_barrier(jnp.max(scores, axis=-1, keepdims=True))
        expo = jnp.where(visible, jnp.exp(scores - row_top), 0.0)
        probs = expo / lax.optimization_barrier(jnp.sum(expo, axis=-1, keepdims=True))
        probs_b = probs.astype(jnp.bfloat16).astype(jnp.float32)
        dprob = jnp.einsum('igad,jgd->gaij', grad_f, values_all)
        delta_t = jnp.transpose(delta_b, (1, 2, 0))[..., None]
        dscore = (probs * (dprob - delta_t)).astype(jnp.bfloat16).astype(jnp.float32)
        query_g = (jnp.einsum('gaij,jgd->igad', dscore, keys_all) * score_scale).astype(jnp.bfloat16)
        key_g = jnp.einsum('gaij,igad->jgd', dscore, query_f) * score_scale
        value_g = jnp.einsum('gaij,igad->jgd', probs_b, grad_f)
        return (query_g, key_g, value_g)
    query_gradient, key_terms, value_terms = lax.map(one_block, (blocked_queries, blocked_keys, key_before, blocked_values, value_before, gradient_blocks, delta_rows, stripe_order, block_ids))
    zeroed_tail = jnp.zeros((1, TAIL_POSITIONS, KEY_HEADS, HEAD_SIZE), jnp.float32)
    key_back = jnp.concatenate([key_terms[1:, BLOCK_TOKENS:], zeroed_tail], axis=0)
    value_back = jnp.concatenate([value_terms[1:, BLOCK_TOKENS:], zeroed_tail], axis=0)
    key_gradient_total = jax.vmap(add_rows)(key_terms[:, :BLOCK_TOKENS], tail_index, key_back)
    value_gradient_total = jax.vmap(add_rows)(value_terms[:, :BLOCK_TOKENS], tail_index, value_back)
    return (query_gradient.reshape(SEQUENCE_LENGTH, QUERY_HEADS * HEAD_SIZE), key_gradient_total.astype(jnp.bfloat16).reshape(SEQUENCE_LENGTH, KEY_HEADS * HEAD_SIZE), value_gradient_total.astype(jnp.bfloat16).reshape(SEQUENCE_LENGTH, KEY_HEADS * HEAD_SIZE))
```

```python
import math

import jax
import jax.numpy as jnp
from jax import lax
from jax.experimental import pallas as pl
from jax.experimental.pallas import tpu as pltpu
from jax.sharding import PartitionSpec as P

HEAD = 128
HEADS = 4
GROUP = 4
ROWS = 128
CHIP_ROWS = 256
BLOCK = 1024
TAIL = 256
KEYS = BLOCK + TAIL
SCALE = 1.0 / math.sqrt(HEAD)
EXP_SCALE = SCALE * math.log2(math.e)
MASKED = -1e30
MESH = pl.DeviceIdType.MESH
F32 = jnp.float32
BF16 = jnp.bfloat16
NN = (((1,), (0,)), ((), ()))
NT = (((1,), (1,)), ((), ()))
TN = (((0,), (0,)), ((), ()))


def dot(a, b, dims=NN):
    return lax.dot_general(a, b, dims, preferred_element_type=F32)


def tile(start, size):
    return pl.ds(pl.multiple_of(start, size), size)


def kernel(
    q_in, k_in, v_in, o_in, g_in, order,
    dq_out, dk_out, dv_out,
    q, g, o, kv, bias, take, give, delta, probs, dscore, acc, dq,
    tail_send, back_send, back_recv, hop_send, hop_recv, out_stage,
    load_sem, own_sem, pair_send, pair_recv,
    first_send, first_recv, sib_send, sib_recv, fwd_send, fwd_recv,
    tail_ssem, tail_rsem, back_ssem, back_rsem, hop_ssem, hop_rsem,
    dq_own, dq_ssem, dq_rsem, kv_own, kv_ssem, kv_rsem,
):
    h = lax.axis_index("head")
    block = lax.axis_index("ctx")
    core = h % 2
    chip = h // 2
    right, left, far = (chip + 1) % 4, (chip + 3) % 4, (chip + 2) % 4
    sib = chip * 2 + 1 - core
    after, before = (block + 1) % 64, (block + 63) % 64
    lo, hi = pl.ds(0, HEAD), pl.ds(HEAD, HEAD)
    right_dev, left_dev, sib_dev = {"head": right * 2 + core}, {"head": left * 2 + core}, {"head": sib}
    after_dev, before_dev = {"ctx": after}, {"ctx": before}
    own_rows = tile(core * ROWS, ROWS)
    sib_rows = tile((1 - core) * ROWS, ROWS)
    wide = GROUP * HEADS * HEAD
    own_cols = tile(core * wide, wide)
    sib_cols = tile((1 - core) * wide, wide)

    def remote(src, dst, ssem, rsem, dev):
        return pltpu.make_async_remote_copy(
            src_ref=src, dst_ref=dst, send_sem=ssem, recv_sem=rsem, device_id=dev, device_id_type=MESH
        )

    def landed(ref, sem):
        pltpu.make_async_copy(ref, ref, sem).wait()

    def chip_rows(c):
        return tile(c * CHIP_ROWS, CHIP_ROWS)

    def block_rows(c, k):
        return tile((c * 2 + k) * ROWS, ROWS)

    def head_cols(k, j):
        return tile((k * HEADS + j) * HEAD, HEAD)

    pairs = ((q_in, q), (g_in, g), (o_in, o))
    loads = [
        pltpu.make_async_copy(src.at[:, own_cols], dst.at[own_rows, :], load_sem.at[i])
        for i, (src, dst) in enumerate(pairs)
    ]
    for c in loads:
        c.start()

    barrier = pltpu.get_barrier_semaphore()
    for dev in (
        {"head": right * 2}, {"head": right * 2 + 1}, {"head": left * 2}, {"head": left * 2 + 1},
        sib_dev, after_dev, before_dev,
    ):
        pl.semaphore_signal(barrier, inc=1, device_id=dev, device_id_type=MESH)
    pl.semaphore_wait(barrier, 7)

    def first_copies(j):
        out = []
        for n, (src, part, to) in enumerate(
            ((k_in, lo, right), (v_in, hi, left), (k_in, lo, left), (v_in, hi, right))
        ):
            for k in range(2):
                out.append(
                    remote(
                        src.at[:, head_cols(k, j)], kv.at[j, block_rows(chip, core), part],
                        first_send.at[j, 2 * n + k], first_recv.at[j, n], {"head": to * 2 + k},
                    )
                )
        return out

    def sib_copies(j):
        return [
            remote(
                src.at[:, head_cols(1 - core, j)], kv.at[j, block_rows(chip, core), part],
                sib_send.at[j, n], sib_recv.at[j], sib_dev,
            )
            for n, (src, part) in enumerate(((k_in, lo), (v_in, hi)))
        ]

    def own_copies(j):
        return [
            pltpu.make_async_copy(
                src.at[:, head_cols(core, j)], kv.at[j, block_rows(chip, core), part], own_sem.at[j, n]
            )
            for n, (src, part) in enumerate(((k_in, lo), (v_in, hi)))
        ]

    def start_first(j):
        for c in first_copies(j) + sib_copies(j) + own_copies(j):
            c.start()

    def fwd_copies(j):
        return (
            remote(kv.at[j, chip_rows(left), lo], kv.at[j, chip_rows(left), lo],
                   fwd_send.at[j, 0], fwd_recv.at[j, 0], right_dev),
            remote(kv.at[j, chip_rows(right), hi], kv.at[j, chip_rows(right), hi],
                   fwd_send.at[j, 1], fwd_recv.at[j, 1], left_dev),
        )

    def forward(j):
        a, b = fwd_copies(j)
        landed(kv.at[j, chip_rows(left), lo], first_recv.at[j, 0])
        a.start()
        landed(kv.at[j, chip_rows(right), hi], first_recv.at[j, 1])
        b.start()

    def gathered(j):
        for c in own_copies(j):
            c.wait()
        landed(kv.at[j, block_rows(chip, 1 - core), :], sib_recv.at[j])
        landed(kv.at[j, chip_rows(right), lo], first_recv.at[j, 2])
        landed(kv.at[j, chip_rows(left), hi], first_recv.at[j, 3])
        landed(kv.at[j, chip_rows(far), lo], fwd_recv.at[j, 0])
        landed(kv.at[j, chip_rows(far), hi], fwd_recv.at[j, 1])

    def tail_copy(j):
        return remote(tail_send.at[j], kv.at[j, pl.ds(BLOCK, TAIL), :], tail_ssem.at[j], tail_rsem.at[j], after_dev)

    def send_tail(j):
        tail_send[j] = dot(take[...], kv[j, :BLOCK, :]).astype(BF16)
        tail_copy(j).start()

    def back_copy(j):
        return remote(back_send.at[j], back_recv.at[j], back_ssem.at[j], back_rsem.at[j], before_dev)

    def hop(j, n):
        dev = right_dev if n in (0, 3, 4) else left_dev
        return remote(hop_send.at[j, n], hop_recv.at[j, n], hop_ssem.at[j, n], hop_rsem.at[j, n], dev)

    def send_hop(j, n, value):
        hop_send[j, n] = value.astype(BF16)
        hop(j, n).start()

    def take_hop(j, n):
        hop(j, n).wait_recv()
        return hop_recv[j, n].astype(F32)

    def hops_first(j):
        s = j % 2
        back_copy(j).wait_recv()
        acc[s, :BLOCK, :] += dot(give[...], back_recv[j])
        send_hop(j, 0, acc[s, chip_rows(far), :HEAD])
        send_hop(j, 1, acc[s, chip_rows(far), HEAD:])
        send_hop(j, 2, acc[s, chip_rows(left), :HEAD])
        send_hop(j, 3, acc[s, chip_rows(right), HEAD:])

    def hops_second(j):
        s = j % 2
        send_hop(j, 4, acc[s, chip_rows(right), :HEAD] + take_hop(j, 0))
        send_hop(j, 5, acc[s, chip_rows(left), HEAD:] + take_hop(j, 1))

    def kv_copies(j):
        own, other = [], []
        for n, (dst, part) in enumerate(((dk_out, lo), (dv_out, hi))):
            cols = head_cols(core, j)
            own.append(pltpu.make_async_copy(out_stage.at[j, own_rows, part], dst.at[:, cols], kv_own.at[j, n]))
            other.append(
                remote(out_stage.at[j, sib_rows, part], dst.at[:, cols], kv_ssem.at[j, n], kv_rsem.at[j, n], sib_dev)
            )
        return own, other

    def hops_last(j):
        s = j % 2
        out_stage[j, :, :HEAD] = (acc[s, chip_rows(chip), :HEAD] + take_hop(j, 2) + take_hop(j, 4)).astype(BF16)
        out_stage[j, :, HEAD:] = (acc[s, chip_rows(chip), HEAD:] + take_hop(j, 3) + take_hop(j, 5)).astype(BF16)
        own, other = kv_copies(j)
        for c in own + other:
            c.start()

    def dq_copies(j):
        cols = tile((core * HEADS + j) * GROUP * HEAD, GROUP * HEAD)
        return (
            pltpu.make_async_copy(dq.at[j, own_rows, :], dq_out.at[:, cols], dq_own.at[j]),
            remote(dq.at[j, sib_rows, :], dq_out.at[:, cols], dq_ssem.at[j], dq_rsem.at[j], sib_dev),
        )

    start_first(0)
    swaps = [
        remote(src.at[:, sib_cols], dst.at[own_rows, :], pair_send.at[i], pair_recv.at[i], sib_dev)
        for i, (src, dst) in enumerate(pairs)
    ]
    for c in swaps:
        c.start()

    order_f = order[...].astype(F32)
    column = jnp.broadcast_to(order_f, (HEAD, BLOCK)).T
    mine = order[:, chip_rows(chip)].astype(F32)
    lane = lax.broadcasted_iota(jnp.int32, (BLOCK, HEAD), 1).astype(F32)
    for half in range(2):
        cols = slice(half * HEAD, (half + 1) * HEAD)
        bias[:BLOCK, cols] = jnp.where(column <= mine[:, cols], 0.0, MASKED)
        give[:, cols] = jnp.where(column == lane + float(BLOCK - TAIL + half * HEAD), 1.0, 0.0).astype(BF16)
    bias[BLOCK:, :] = jnp.full((TAIL, CHIP_ROWS), jnp.where(block > 0, 0.0, MASKED), F32)
    place = lax.broadcasted_iota(jnp.int32, (TAIL, BLOCK), 0).astype(F32)
    take[...] = jnp.where(order_f == place + float(BLOCK - TAIL), 1.0, 0.0).astype(BF16)

    forward(0)
    start_first(1)

    for c in loads:
        c.wait()
    for c in swaps:
        c.wait_recv()

    def delta_of(n, _):
        cols = tile(n * HEAD, HEAD)
        product = o[:, cols].astype(F32) * g[:, cols].astype(F32)
        delta[n] = jnp.sum(product.T, axis=0, keepdims=True)
        return 0

    lax.fori_loop(0, GROUP * HEADS, delta_of, 0)

    gathered(0)
    send_tail(0)
    forward(1)
    start_first(2)

    def step(n, _):
        j = n // GROUP
        a = n % GROUP

        @pl.when(a == 0)
        def _():
            tail_copy(j).wait_recv()

        cols = tile(n * HEAD, HEAD)
        lanes = tile(a * CHIP_ROWS, CHIP_ROWS)
        keys = kv[j, :, :HEAD]
        values = kv[j, :, HEAD:]
        s = dot(keys, q[:, cols], NT) + bias[...]
        top = jnp.max(s, axis=0, keepdims=True)
        e = jnp.exp2((s - top) * EXP_SCALE)
        p = e * (1.0 / jnp.sum(e, axis=0, keepdims=True))
        probs[:, lanes] = p.astype(BF16)
        dp = dot(values, g[:, cols], NT)
        ds = (p * (dp - delta[n])).astype(BF16)
        dscore[:, lanes] = ds
        dq[j, :, tile(a * HEAD, HEAD)] = (dot(ds, keys, TN) * SCALE).astype(BF16)

        @pl.when((a == 0) & (j >= 1))
        def _():
            hops_first(j - 1)

        @pl.when((a == 1) & (j == 0))
        def _():
            start_first(3)

        @pl.when((a == 2) & (j >= 1))
        def _():
            hops_second(j - 1)

        @pl.when((a == 2) & (j <= 2))
        def _():
            gathered(j + 1)
            send_tail(j + 1)

            @pl.when(j <= 1)
            def _():
                forward(j + 2)

        @pl.when(a == 3)
        def _():
            s = j % 2
            wide_q = tile(j * GROUP * HEAD, GROUP * HEAD)
            qs = q[:, wide_q]
            gs = g[:, wide_q]
            rows_q = jnp.concatenate([qs[:, i * HEAD : (i + 1) * HEAD] for i in range(GROUP)], axis=0)
            rows_g = jnp.concatenate([gs[:, i * HEAD : (i + 1) * HEAD] for i in range(GROUP)], axis=0)
            acc[s, :, :HEAD] = dot(dscore[...], rows_q) * SCALE
            acc[s, :, HEAD:] = dot(probs[...], rows_g)
            back_send[j] = acc[s, BLOCK:, :].astype(BF16)
            back_copy(j).start()
            for c in dq_copies(j):
                c.start()

            @pl.when(j >= 1)
            def _():
                hops_last(j - 1)

        return 0

    lax.fori_loop(0, GROUP * HEADS, step, 0)
    hops_first(HEADS - 1)
    hops_second(HEADS - 1)
    hops_last(HEADS - 1)

    for c in swaps:
        c.wait_send()

    def finish(j, _):
        for c in first_copies(j) + sib_copies(j):
            c.wait_send()
        for c in fwd_copies(j):
            c.wait_send()
        tail_copy(j).wait_send()
        back_copy(j).wait_send()
        for n in range(6):
            hop(j, n).wait_send()
        own, other = dq_copies(j)
        own.wait()
        other.wait()
        own, other = kv_copies(j)
        for c in own + other:
            c.wait()
        return 0

    lax.fori_loop(0, HEADS, finish, 0)


def body(queries, keys, values, output, gradient, order):
    any_spec = pl.BlockSpec(memory_space=pl.ANY)
    wide = GROUP * HEADS * HEAD
    dma = pltpu.SemaphoreType.DMA
    return pl.pallas_call(
        kernel,
        out_shape=(
            jax.ShapeDtypeStruct(queries.shape, BF16),
            jax.ShapeDtypeStruct(keys.shape, BF16),
            jax.ShapeDtypeStruct(values.shape, BF16),
        ),
        in_specs=[any_spec] * 5 + [pl.BlockSpec(memory_space=pltpu.VMEM)],
        out_specs=[any_spec] * 3,
        scratch_shapes=[
            pltpu.VMEM((CHIP_ROWS, wide), BF16),
            pltpu.VMEM((CHIP_ROWS, wide), BF16),
            pltpu.VMEM((CHIP_ROWS, wide), BF16),
            pltpu.VMEM((HEADS, KEYS, 2 * HEAD), BF16),
            pltpu.VMEM((KEYS, CHIP_ROWS), F32),
            pltpu.VMEM((TAIL, BLOCK), BF16),
            pltpu.VMEM((BLOCK, TAIL), BF16),
            pltpu.VMEM((GROUP * HEADS, 1, CHIP_ROWS), F32),
            pltpu.VMEM((KEYS, GROUP * CHIP_ROWS), BF16),
            pltpu.VMEM((KEYS, GROUP * CHIP_ROWS), BF16),
            pltpu.VMEM((2, KEYS, 2 * HEAD), F32),
            pltpu.VMEM((HEADS, CHIP_ROWS, GROUP * HEAD), BF16),
            pltpu.VMEM((HEADS, TAIL, 2 * HEAD), BF16),
            pltpu.VMEM((HEADS, TAIL, 2 * HEAD), BF16),
            pltpu.VMEM((HEADS, TAIL, 2 * HEAD), BF16),
            pltpu.VMEM((HEADS, 6, CHIP_ROWS, HEAD), BF16),
            pltpu.VMEM((HEADS, 6, CHIP_ROWS, HEAD), BF16),
            pltpu.VMEM((HEADS, CHIP_ROWS, 2 * HEAD), BF16),
            dma((3,)), dma((HEADS, 2)), dma((3,)), dma((3,)),
            dma((HEADS, 8)), dma((HEADS, 4)), dma((HEADS, 2)), dma((HEADS,)), dma((HEADS, 2)), dma((HEADS, 2)),
            dma((HEADS,)), dma((HEADS,)), dma((HEADS,)), dma((HEADS,)), dma((HEADS, 6)), dma((HEADS, 6)),
            dma((HEADS,)), dma((HEADS,)), dma((HEADS,)), dma((HEADS, 2)), dma((HEADS, 2)), dma((HEADS, 2)),
        ],
        compiler_params=pltpu.CompilerParams(
            collective_id=0, has_side_effects=True, vmem_limit_bytes=48 * 2**20
        ),
        name="banded_attention_grad",
    )(queries, keys, values, output, gradient, order)


def solution(mesh):
    spec = P(("ctx", "head"), None)
    return jax.shard_map(
        body,
        mesh=mesh,
        in_specs=(spec,) * 5 + (P("ctx", None),),
        out_specs=(spec,) * 3,
        check_vma=False,
    )
```

```python
import math

import jax
import jax.numpy as jnp
from jax import lax
from jax.experimental import pallas as pl
from jax.experimental.pallas import tpu as pltpu
from jax.sharding import PartitionSpec as P

HEAD = 128
HEADS = 4
GROUP = 4
ROWS = 128
CHIP_ROWS = 256
BLOCK = 1024
TAIL = 256
KEYS = BLOCK + TAIL
PART = 256
SCALE = 1.0 / math.sqrt(HEAD)
EXP_SCALE = SCALE * math.log2(math.e)
MASKED = -1e30
MESH = pl.DeviceIdType.MESH
F32 = jnp.float32
BF16 = jnp.bfloat16
NN = (((1,), (0,)), ((), ()))
NT = (((1,), (1,)), ((), ()))
TN = (((0,), (0,)), ((), ()))


def dot(a, b, dims=NN):
    return lax.dot_general(a, b, dims, preferred_element_type=F32)


def tile(start, size):
    return pl.ds(pl.multiple_of(start, size), size)


def kernel(
    q_in, k_in, v_in, o_in, g_in, order,
    dq_out, dk_out, dv_out,
    q, g, o, kv, bias, take, give, delta, scores, keys_t, probs, dscore, acc, dq,
    tail_send, back_send, back_recv, hop_send, hop_recv, out_stage,
    load_sem, own_sem, pair_send, pair_recv,
    first_send, first_recv, sib_send, sib_recv, fwd_send, fwd_recv,
    tail_ssem, tail_rsem, back_ssem, back_rsem, hop_ssem, hop_rsem,
    dq_own, dq_ssem, dq_rsem, kv_own, kv_ssem, kv_rsem,
):
    h = lax.axis_index("head")
    block = lax.axis_index("ctx")
    core = h % 2
    chip = h // 2
    right, left, far = (chip + 1) % 4, (chip + 3) % 4, (chip + 2) % 4
    sib = chip * 2 + 1 - core
    after, before = (block + 1) % 64, (block + 63) % 64
    bend_after = (block % 8 + 1) // 8 * (block // 8 % 2 * 2 - 1)
    bend_before = (before % 8 + 1) // 8 * (before // 8 % 2 * 2 - 1)
    lo, hi = pl.ds(0, HEAD), pl.ds(HEAD, HEAD)
    right_dev, left_dev, sib_dev = {"head": right * 2 + core}, {"head": left * 2 + core}, {"head": sib}

    def after_dev(n):
        return {"head": (chip + 4 + n * bend_after) % 4 * 2 + core, "ctx": after}

    def before_dev(n):
        return {"head": (chip + 4 - n * bend_before) % 4 * 2 + core, "ctx": before}

    own_rows = tile(core * ROWS, ROWS)
    sib_rows = tile((1 - core) * ROWS, ROWS)
    wide = GROUP * HEADS * HEAD
    own_cols = tile(core * wide, wide)
    sib_cols = tile((1 - core) * wide, wide)

    def remote(src, dst, ssem, rsem, dev):
        return pltpu.make_async_remote_copy(
            src_ref=src, dst_ref=dst, send_sem=ssem, recv_sem=rsem, device_id=dev, device_id_type=MESH
        )

    def landed(ref, sem):
        pltpu.make_async_copy(ref, ref, sem).wait()

    def chip_rows(c):
        return tile(c * CHIP_ROWS, CHIP_ROWS)

    def block_rows(c, k):
        return tile((c * 2 + k) * ROWS, ROWS)

    def head_cols(k, j):
        return tile((k * HEADS + j) * HEAD, HEAD)

    pairs = ((q_in, q), (g_in, g), (o_in, o))
    loads = [
        pltpu.make_async_copy(src.at[:, own_cols], dst.at[own_rows, :], load_sem.at[i])
        for i, (src, dst) in enumerate(pairs)
    ]
    for c in loads:
        c.start()

    barrier = pltpu.get_barrier_semaphore()
    for dev in (
        {"head": right * 2}, {"head": right * 2 + 1}, {"head": left * 2}, {"head": left * 2 + 1},
        sib_dev, before_dev(0), before_dev(1),
    ):
        pl.semaphore_signal(barrier, inc=1, device_id=dev, device_id_type=MESH)
    pl.semaphore_wait(barrier, 7)

    def first_copies(j):
        out = []
        for n, (src, part, to) in enumerate(
            ((k_in, lo, right), (v_in, hi, left), (k_in, lo, left), (v_in, hi, right))
        ):
            for k in range(2):
                out.append(
                    remote(
                        src.at[:, head_cols(k, j)], kv.at[j, block_rows(chip, core), part],
                        first_send.at[j, 2 * n + k], first_recv.at[j, n], {"head": to * 2 + k},
                    )
                )
        return out

    def sib_copies(j):
        return [
            remote(
                src.at[:, head_cols(1 - core, j)], kv.at[j, block_rows(chip, core), part],
                sib_send.at[j, n], sib_recv.at[j], sib_dev,
            )
            for n, (src, part) in enumerate(((k_in, lo), (v_in, hi)))
        ]

    def own_copies(j):
        return [
            pltpu.make_async_copy(
                src.at[:, head_cols(core, j)], kv.at[j, block_rows(chip, core), part], own_sem.at[j, n]
            )
            for n, (src, part) in enumerate(((k_in, lo), (v_in, hi)))
        ]

    def start_first(j):
        for c in first_copies(j) + sib_copies(j) + own_copies(j):
            c.start()

    def fwd_copies(j):
        return (
            remote(kv.at[j, chip_rows(left), lo], kv.at[j, chip_rows(left), lo],
                   fwd_send.at[j, 0], fwd_recv.at[j, 0], right_dev),
            remote(kv.at[j, chip_rows(right), hi], kv.at[j, chip_rows(right), hi],
                   fwd_send.at[j, 1], fwd_recv.at[j, 1], left_dev),
        )

    def forward(j):
        a, b = fwd_copies(j)
        landed(kv.at[j, chip_rows(left), lo], first_recv.at[j, 0])
        a.start()
        landed(kv.at[j, chip_rows(right), hi], first_recv.at[j, 1])
        b.start()

    def gathered(j):
        for c in own_copies(j):
            c.wait()
        landed(kv.at[j, block_rows(chip, 1 - core), :], sib_recv.at[j])
        landed(kv.at[j, chip_rows(right), lo], first_recv.at[j, 2])
        landed(kv.at[j, chip_rows(left), hi], first_recv.at[j, 3])
        landed(kv.at[j, chip_rows(far), lo], fwd_recv.at[j, 0])
        landed(kv.at[j, chip_rows(far), hi], fwd_recv.at[j, 1])

    halves = (slice(0, HEAD), slice(HEAD, 2 * HEAD))

    def tail_copies(j):
        return [
            remote(tail_send.at[j, n], kv.at[j, pl.ds(BLOCK, TAIL), part],
                   tail_ssem.at[j, n], tail_rsem.at[j, n], after_dev(n))
            for n, part in enumerate((lo, hi))
        ]

    def send_tail(j):
        rows = dot(take[...], kv[j, :BLOCK, :]).astype(BF16)
        for n, c in enumerate(tail_copies(j)):
            tail_send[j, n] = rows[:, halves[n]]
            c.start()

    def back_copies(j):
        return [
            remote(back_send.at[j, n], back_recv.at[j, n], back_ssem.at[j, n], back_rsem.at[j, n], before_dev(n))
            for n in range(2)
        ]

    def hop(j, n):
        dev = right_dev if n in (0, 3, 4) else left_dev
        return remote(hop_send.at[j, n], hop_recv.at[j, n], hop_ssem.at[j, n], hop_rsem.at[j, n], dev)

    def send_hop(j, n, value):
        hop_send[j, n] = value.astype(BF16)
        hop(j, n).start()

    def take_hop(j, n):
        hop(j, n).wait_recv()
        return hop_recv[j, n].astype(F32)

    def hops_first(j):
        s = j
        for c in back_copies(j):
            c.wait_recv()
        back = jnp.concatenate([back_recv[j, 0], back_recv[j, 1]], axis=1)
        acc[s] += dot(give[...], back)
        send_hop(j, 0, acc[s, chip_rows(far), :HEAD])
        send_hop(j, 1, acc[s, chip_rows(far), HEAD:])
        send_hop(j, 2, acc[s, chip_rows(left), :HEAD])
        send_hop(j, 3, acc[s, chip_rows(right), HEAD:])

    def hops_second(j):
        s = j
        send_hop(j, 4, acc[s, chip_rows(right), :HEAD] + take_hop(j, 0))
        send_hop(j, 5, acc[s, chip_rows(left), HEAD:] + take_hop(j, 1))

    def kv_copies(j):
        own, other = [], []
        for n, (dst, part) in enumerate(((dk_out, lo), (dv_out, hi))):
            cols = head_cols(core, j)
            own.append(pltpu.make_async_copy(out_stage.at[j, own_rows, part], dst.at[:, cols], kv_own.at[j, n]))
            other.append(
                remote(out_stage.at[j, sib_rows, part], dst.at[:, cols], kv_ssem.at[j, n], kv_rsem.at[j, n], sib_dev)
            )
        return own, other

    def hops_last(j):
        s = j
        out_stage[j, :, :HEAD] = (acc[s, chip_rows(chip), :HEAD] + take_hop(j, 2) + take_hop(j, 4)).astype(BF16)
        out_stage[j, :, HEAD:] = (acc[s, chip_rows(chip), HEAD:] + take_hop(j, 3) + take_hop(j, 5)).astype(BF16)
        own, other = kv_copies(j)
        for c in own + other:
            c.start()

    def dq_copies(j):
        cols = tile((core * HEADS + j) * GROUP * HEAD, GROUP * HEAD)
        return (
            pltpu.make_async_copy(dq.at[j, own_rows, :], dq_out.at[:, cols], dq_own.at[j]),
            remote(dq.at[j, sib_rows, :], dq_out.at[:, cols], dq_ssem.at[j], dq_rsem.at[j], sib_dev),
        )

    start_first(0)
    swaps = [
        remote(src.at[:, sib_cols], dst.at[own_rows, :], pair_send.at[i], pair_recv.at[i], sib_dev)
        for i, (src, dst) in enumerate(pairs)
    ]
    for c in swaps:
        c.start()

    order_f = order[...].astype(F32)
    place = lax.broadcasted_iota(jnp.int32, (TAIL, BLOCK), 0).astype(F32)
    take[...] = jnp.where(order_f == place + float(BLOCK - TAIL), 1.0, 0.0).astype(BF16)
    column = jnp.broadcast_to(order_f, (HEAD, BLOCK)).T
    mine = order[:, chip_rows(chip)].astype(F32)
    lane = lax.broadcasted_iota(jnp.int32, (BLOCK, HEAD), 1).astype(F32)
    for half in range(2):
        cols = slice(half * HEAD, (half + 1) * HEAD)
        bias[:BLOCK, cols] = jnp.where(column <= mine[:, cols], 0.0, MASKED)
        give[:, cols] = jnp.where(column == lane + float(BLOCK - TAIL + half * HEAD), 1.0, 0.0).astype(BF16)
    bias[BLOCK:, :] = jnp.full((TAIL, CHIP_ROWS), jnp.where(block > 0, 0.0, MASKED), F32)

    forward(0)
    start_first(1)

    for c in loads:
        c.wait()
    for c in swaps:
        c.wait_recv()

    def delta_of(n, _):
        cols = tile(n * HEAD, HEAD)
        product = o[:, cols].astype(F32) * g[:, cols].astype(F32)
        delta[n] = jnp.sum(product.T, axis=0, keepdims=True)
        return 0

    lax.fori_loop(0, GROUP * HEADS, delta_of, 0)

    gathered(0)
    send_tail(0)
    start_first(2)
    forward(1)
    start_first(3)
    gathered(1)
    send_tail(1)
    forward(2)

    def step(j, _):
        for c in tail_copies(j):
            c.wait_recv()
        keys_t[...] = kv[j, :, :HEAD].T
        for a in range(GROUP):
            n = j * GROUP + a
            cols = tile(n * HEAD, HEAD)
            lanes = slice(a * CHIP_ROWS, (a + 1) * CHIP_ROWS)
            u = a % 2
            query = q[:, cols]
            top = None
            for t in range(KEYS // PART):
                r = slice(t * PART, (t + 1) * PART)
                part = dot(kv[j, r, :HEAD], query, NT) + bias[r, :]
                scores[u, r, :] = part
                part = jnp.max(part.reshape(PART // 8, 8, CHIP_ROWS), axis=0)
                top = part if top is None else jnp.maximum(top, part)
            top = jnp.max(top, axis=0, keepdims=True)
            total = None
            for t in range(KEYS // PART):
                r = slice(t * PART, (t + 1) * PART)
                part = jnp.exp2((scores[u, r, :] - top) * EXP_SCALE)
                scores[u, r, :] = part
                part = jnp.sum(part.reshape(PART // 8, 8, CHIP_ROWS), axis=0)
                total = part if total is None else total + part
            share = 1.0 / jnp.sum(total, axis=0, keepdims=True)
            grad = g[:, cols]
            shift = delta[n]
            for t in range(KEYS // PART):
                r = slice(t * PART, (t + 1) * PART)
                p = scores[u, r, :] * share
                probs[r, lanes] = p.astype(BF16)
                dp = dot(kv[j, r, HEAD:], grad, NT)
                dscore[r, lanes] = (p * (dp - shift)).astype(BF16)
        wide_q = tile(j * GROUP * HEAD, GROUP * HEAD)
        qs = q[:, wide_q]
        gs = g[:, wide_q]
        rows_q = jnp.concatenate([qs[:, i * HEAD : (i + 1) * HEAD] for i in range(GROUP)], axis=0)
        rows_g = jnp.concatenate([gs[:, i * HEAD : (i + 1) * HEAD] for i in range(GROUP)], axis=0)
        back_send[j, 0] = (dot(dscore[BLOCK:, :], rows_q) * SCALE).astype(BF16)
        back_send[j, 1] = dot(probs[BLOCK:, :], rows_g).astype(BF16)
        for c in back_copies(j):
            c.start()
        acc[j, :, :HEAD] = dot(dscore[:BLOCK, :], rows_q) * SCALE
        acc[j, :, HEAD:] = dot(probs[:BLOCK, :], rows_g)
        dq_t = dot(keys_t[...], dscore[...])
        for a in range(GROUP):
            dq[j, :, a * HEAD : (a + 1) * HEAD] = (dq_t[:, a * CHIP_ROWS : (a + 1) * CHIP_ROWS].T * SCALE).astype(BF16)
        for c in dq_copies(j):
            c.start()

        @pl.when(j == 0)
        def _():
            forward(3)

        @pl.when((j == 0) | (j == 2))
        def _():
            gathered(j // 2 + 2)
            send_tail(j // 2 + 2)

        @pl.when(j >= 1)
        def _():
            hops_first(j - 1)

        return 0

    lax.fori_loop(0, HEADS, step, 0)
    hops_second(0)
    hops_second(1)
    hops_first(3)
    hops_last(0)
    hops_second(2)
    hops_last(1)
    hops_second(3)
    hops_last(2)
    hops_last(3)

    for c in swaps:
        c.wait_send()

    def finish(j, _):
        for c in first_copies(j) + sib_copies(j):
            c.wait_send()
        for c in fwd_copies(j):
            c.wait_send()
        for c in tail_copies(j) + back_copies(j):
            c.wait_send()
        for n in range(6):
            hop(j, n).wait_send()
        own, other = dq_copies(j)
        own.wait()
        other.wait()
        own, other = kv_copies(j)
        for c in own + other:
            c.wait()
        return 0

    lax.fori_loop(0, HEADS, finish, 0)


def body(queries, keys, values, output, gradient, order):
    any_spec = pl.BlockSpec(memory_space=pl.ANY)
    wide = GROUP * HEADS * HEAD
    dma = pltpu.SemaphoreType.DMA
    return pl.pallas_call(
        kernel,
        out_shape=(
            jax.ShapeDtypeStruct(queries.shape, BF16),
            jax.ShapeDtypeStruct(keys.shape, BF16),
            jax.ShapeDtypeStruct(values.shape, BF16),
        ),
        in_specs=[any_spec] * 5 + [pl.BlockSpec(memory_space=pltpu.VMEM)],
        out_specs=[any_spec] * 3,
        scratch_shapes=[
            pltpu.VMEM((CHIP_ROWS, wide), BF16),
            pltpu.VMEM((CHIP_ROWS, wide), BF16),
            pltpu.VMEM((CHIP_ROWS, wide), BF16),
            pltpu.VMEM((HEADS, KEYS, 2 * HEAD), BF16),
            pltpu.VMEM((KEYS, CHIP_ROWS), F32),
            pltpu.VMEM((TAIL, BLOCK), BF16),
            pltpu.VMEM((BLOCK, TAIL), BF16),
            pltpu.VMEM((GROUP * HEADS, 1, CHIP_ROWS), F32),
            pltpu.VMEM((2, KEYS, CHIP_ROWS), F32),
            pltpu.VMEM((HEAD, KEYS), BF16),
            pltpu.VMEM((KEYS, GROUP * CHIP_ROWS), BF16),
            pltpu.VMEM((KEYS, GROUP * CHIP_ROWS), BF16),
            pltpu.VMEM((HEADS, BLOCK, 2 * HEAD), F32),
            pltpu.VMEM((HEADS, CHIP_ROWS, GROUP * HEAD), BF16),
            pltpu.VMEM((HEADS, 2, TAIL, HEAD), BF16),
            pltpu.VMEM((HEADS, 2, TAIL, HEAD), BF16),
            pltpu.VMEM((HEADS, 2, TAIL, HEAD), BF16),
            pltpu.VMEM((HEADS, 6, CHIP_ROWS, HEAD), BF16),
            pltpu.VMEM((HEADS, 6, CHIP_ROWS, HEAD), BF16),
            pltpu.VMEM((HEADS, CHIP_ROWS, 2 * HEAD), BF16),
            dma((3,)), dma((HEADS, 2)), dma((3,)), dma((3,)),
            dma((HEADS, 8)), dma((HEADS, 4)), dma((HEADS, 2)), dma((HEADS,)), dma((HEADS, 2)), dma((HEADS, 2)),
            dma((HEADS, 2)), dma((HEADS, 2)), dma((HEADS, 2)), dma((HEADS, 2)), dma((HEADS, 6)), dma((HEADS, 6)),
            dma((HEADS,)), dma((HEADS,)), dma((HEADS,)), dma((HEADS, 2)), dma((HEADS, 2)), dma((HEADS, 2)),
        ],
        compiler_params=pltpu.CompilerParams(
            collective_id=0, has_side_effects=True, vmem_limit_bytes=62 * 2**20
        ),
        name="banded_attention_grad",
    )(queries, keys, values, output, gradient, order)


def solution(mesh):
    spec = P(("ctx", "head"), None)
    return jax.shard_map(
        body,
        mesh=mesh,
        in_specs=(spec,) * 5 + (P("ctx", None),),
        out_specs=(spec,) * 3,
        check_vma=False,
    )
```

```python
import math

import jax
import jax.numpy as jnp
from jax import lax
from jax.experimental import pallas as pl
from jax.experimental.pallas import tpu as pltpu
from jax.sharding import PartitionSpec as P

HEAD = 128
HEADS = 4
GROUP = 4
ROWS = 128
CHIP_ROWS = 256
BLOCK = 1024
TAIL = 256
KEYS = BLOCK + TAIL
PART = 256
SCALE = 1.0 / math.sqrt(HEAD)
EXP_SCALE = SCALE * math.log2(math.e)
MASKED = -1e30
MESH = pl.DeviceIdType.MESH
F32 = jnp.float32
BF16 = jnp.bfloat16
NN = (((1,), (0,)), ((), ()))
NT = (((1,), (1,)), ((), ()))
TN = (((0,), (0,)), ((), ()))


def dot(a, b, dims=NN):
    return lax.dot_general(a, b, dims, preferred_element_type=F32)


def tile(start, size):
    return pl.ds(pl.multiple_of(start, size), size)


def kernel(
    q_in, k_in, v_in, o_in, g_in, order,
    dq_out, dk_out, dv_out,
    q, g, o, kv, bias, take, give, delta, scores, keys_t, probs, dscore, acc, dq,
    tail_send, back_send, back_recv, hop_send, hop_recv, out_stage,
    load_sem, own_sem, pair_send, pair_recv,
    first_send, first_recv, sib_send, sib_recv, fwd_send, fwd_recv,
    tail_ssem, tail_rsem, back_ssem, back_rsem, hop_ssem, hop_rsem,
    dq_own, dq_ssem, dq_rsem, kv_own, kv_ssem, kv_rsem,
):
    h = lax.axis_index("head")
    block = lax.axis_index("ctx")
    core = h % 2
    chip = h // 2
    right, left, far = (chip + 1) % 4, (chip + 3) % 4, (chip + 2) % 4
    sib = chip * 2 + 1 - core
    after, before = (block + 1) % 64, (block + 63) % 64
    bend_after = (block % 8 + 1) // 8 * (block // 8 % 2 * 2 - 1)
    bend_before = (before % 8 + 1) // 8 * (before // 8 % 2 * 2 - 1)
    eager = 1 - (block % 8 + 7) // 8
    lo, hi = pl.ds(0, HEAD), pl.ds(HEAD, HEAD)
    right_dev, left_dev, sib_dev = {"head": right * 2 + core}, {"head": left * 2 + core}, {"head": sib}

    def after_dev(n):
        return {"head": (chip + 4 + n * bend_after) % 4 * 2 + core, "ctx": after}

    def before_dev(n):
        return {"head": (chip + 4 - n * bend_before) % 4 * 2 + core, "ctx": before}

    own_rows = tile(core * ROWS, ROWS)
    sib_rows = tile((1 - core) * ROWS, ROWS)
    wide = GROUP * HEADS * HEAD
    own_cols = tile(core * wide, wide)
    sib_cols = tile((1 - core) * wide, wide)

    def remote(src, dst, ssem, rsem, dev):
        return pltpu.make_async_remote_copy(
            src_ref=src, dst_ref=dst, send_sem=ssem, recv_sem=rsem, device_id=dev, device_id_type=MESH
        )

    def landed(ref, sem):
        pltpu.make_async_copy(ref, ref, sem).wait()

    def chip_rows(c):
        return tile(c * CHIP_ROWS, CHIP_ROWS)

    def block_rows(c, k):
        return tile((c * 2 + k) * ROWS, ROWS)

    def head_cols(k, j):
        return tile((k * HEADS + j) * HEAD, HEAD)

    pairs = ((q_in, q), (g_in, g), (o_in, o))
    loads = [
        pltpu.make_async_copy(src.at[:, own_cols], dst.at[own_rows, :], load_sem.at[i])
        for i, (src, dst) in enumerate(pairs)
    ]
    for c in loads:
        c.start()

    barrier = pltpu.get_barrier_semaphore()
    for dev in (
        {"head": right * 2}, {"head": right * 2 + 1}, {"head": left * 2}, {"head": left * 2 + 1},
        sib_dev, before_dev(0), before_dev(1),
    ):
        pl.semaphore_signal(barrier, inc=1, device_id=dev, device_id_type=MESH)
    pl.semaphore_wait(barrier, 7)

    def first_copies(j, which=(0, 1, 2, 3)):
        kinds = ((k_in, lo, right), (v_in, hi, left), (k_in, lo, left), (v_in, hi, right))
        out = []
        for n in which:
            src, part, to = kinds[n]
            for k in range(2):
                out.append(
                    remote(
                        src.at[:, head_cols(k, j)], kv.at[j, block_rows(chip, core), part],
                        first_send.at[j, 2 * n + k], first_recv.at[j, n], {"head": to * 2 + k},
                    )
                )
        return out

    def sib_copies(j):
        return [
            remote(
                src.at[:, head_cols(1 - core, j)], kv.at[j, block_rows(chip, core), part],
                sib_send.at[j, n], sib_recv.at[j], sib_dev,
            )
            for n, (src, part) in enumerate(((k_in, lo), (v_in, hi)))
        ]

    def own_copies(j):
        return [
            pltpu.make_async_copy(
                src.at[:, head_cols(core, j)], kv.at[j, block_rows(chip, core), part], own_sem.at[j, n]
            )
            for n, (src, part) in enumerate(((k_in, lo), (v_in, hi)))
        ]

    def start_onward(j):
        for c in first_copies(j, (0, 1)) + sib_copies(j) + own_copies(j):
            c.start()

    def start_near(j):
        for c in first_copies(j, (2, 3)):
            c.start()

    def fwd_copies(j):
        return (
            remote(kv.at[j, chip_rows(left), lo], kv.at[j, chip_rows(left), lo],
                   fwd_send.at[j, 0], fwd_recv.at[j, 0], right_dev),
            remote(kv.at[j, chip_rows(right), hi], kv.at[j, chip_rows(right), hi],
                   fwd_send.at[j, 1], fwd_recv.at[j, 1], left_dev),
        )

    def forward(j):
        a, b = fwd_copies(j)
        landed(kv.at[j, chip_rows(left), lo], first_recv.at[j, 0])
        a.start()
        landed(kv.at[j, chip_rows(right), hi], first_recv.at[j, 1])
        b.start()

    def gathered(j):
        for c in own_copies(j):
            c.wait()
        landed(kv.at[j, block_rows(chip, 1 - core), :], sib_recv.at[j])
        landed(kv.at[j, chip_rows(right), lo], first_recv.at[j, 2])
        landed(kv.at[j, chip_rows(left), hi], first_recv.at[j, 3])
        landed(kv.at[j, chip_rows(far), lo], fwd_recv.at[j, 0])
        landed(kv.at[j, chip_rows(far), hi], fwd_recv.at[j, 1])

    halves = (slice(0, HEAD), slice(HEAD, 2 * HEAD))

    def tail_copies(j):
        return [
            remote(tail_send.at[j, n], kv.at[j, pl.ds(BLOCK, TAIL), part],
                   tail_ssem.at[j, n], tail_rsem.at[j, n], after_dev(n))
            for n, part in enumerate((lo, hi))
        ]

    def send_tail(j):
        rows = dot(take[...], kv[j, :BLOCK, :]).astype(BF16)
        for n, c in enumerate(tail_copies(j)):
            tail_send[j, n] = rows[:, halves[n]]
            c.start()

    def back_copies(j):
        return [
            remote(back_send.at[j, n], back_recv.at[j, n], back_ssem.at[j, n], back_rsem.at[j, n], before_dev(n))
            for n in range(2)
        ]

    def hop(j, n):
        dev = right_dev if n in (0, 3, 4) else left_dev
        return remote(hop_send.at[j, n], hop_recv.at[j, n], hop_ssem.at[j, n], hop_rsem.at[j, n], dev)

    def send_hop(j, n, value):
        hop_send[j, n] = value.astype(BF16)
        hop(j, n).start()

    def take_hop(j, n):
        hop(j, n).wait_recv()
        return hop_recv[j, n].astype(F32)

    def hops_first(j):
        for c in back_copies(j):
            c.wait_recv()
        back = jnp.concatenate([back_recv[j, 0], back_recv[j, 1]], axis=1)

        def whole(c):
            return acc[j, chip_rows(c), :] + dot(give[chip_rows(c), :], back)

        part = whole(far)
        send_hop(j, 0, part[:, :HEAD])
        send_hop(j, 1, part[:, HEAD:])
        part = whole(left)
        send_hop(j, 2, part[:, :HEAD])
        acc[j, chip_rows(left), HEAD:] = part[:, HEAD:]
        part = whole(right)
        send_hop(j, 3, part[:, HEAD:])
        acc[j, chip_rows(right), :HEAD] = part[:, :HEAD]
        acc[j, chip_rows(chip), :] = whole(chip)

    def hops_second(j):
        s = j
        send_hop(j, 4, acc[s, chip_rows(right), :HEAD] + take_hop(j, 0))
        send_hop(j, 5, acc[s, chip_rows(left), HEAD:] + take_hop(j, 1))

    def kv_copies(j):
        own, other = [], []
        for n, (dst, part) in enumerate(((dk_out, lo), (dv_out, hi))):
            cols = head_cols(core, j)
            own.append(pltpu.make_async_copy(out_stage.at[j, own_rows, part], dst.at[:, cols], kv_own.at[j, n]))
            other.append(
                remote(out_stage.at[j, sib_rows, part], dst.at[:, cols], kv_ssem.at[j, n], kv_rsem.at[j, n], sib_dev)
            )
        return own, other

    def hops_last(j):
        s = j
        out_stage[j, :, :HEAD] = (acc[s, chip_rows(chip), :HEAD] + take_hop(j, 2) + take_hop(j, 4)).astype(BF16)
        out_stage[j, :, HEAD:] = (acc[s, chip_rows(chip), HEAD:] + take_hop(j, 3) + take_hop(j, 5)).astype(BF16)
        own, other = kv_copies(j)
        for c in own + other:
            c.start()

    def dq_copies(j):
        cols = tile((core * HEADS + j) * GROUP * HEAD, GROUP * HEAD)
        return (
            pltpu.make_async_copy(dq.at[j, own_rows, :], dq_out.at[:, cols], dq_own.at[j]),
            remote(dq.at[j, sib_rows, :], dq_out.at[:, cols], dq_ssem.at[j], dq_rsem.at[j], sib_dev),
        )

    start_onward(0)
    start_near(0)
    swaps = [
        remote(src.at[:, sib_cols], dst.at[own_rows, :], pair_send.at[i], pair_recv.at[i], sib_dev)
        for i, (src, dst) in enumerate(pairs)
    ]
    for c in swaps:
        c.start()
    start_onward(1)

    order_f = order[...].astype(F32)
    place = lax.broadcasted_iota(jnp.int32, (TAIL, BLOCK), 0).astype(F32)
    take[...] = jnp.where(order_f == place + float(BLOCK - TAIL), 1.0, 0.0).astype(BF16)

    forward(0)
    start_near(1)
    start_onward(2)

    column = jnp.broadcast_to(order_f, (HEAD, BLOCK)).T
    mine = order[:, chip_rows(chip)].astype(F32)
    lane = lax.broadcasted_iota(jnp.int32, (BLOCK, HEAD), 1).astype(F32)
    for half in range(2):
        cols = slice(half * HEAD, (half + 1) * HEAD)
        bias[:BLOCK, cols] = jnp.where(column <= mine[:, cols], 0.0, MASKED)
        give[:, cols] = jnp.where(column == lane + float(BLOCK - TAIL + half * HEAD), 1.0, 0.0).astype(BF16)
    bias[BLOCK:, :] = jnp.full((TAIL, CHIP_ROWS), jnp.where(block > 0, 0.0, MASKED), F32)

    gathered(0)
    send_tail(0)
    forward(1)
    start_near(2)
    start_onward(3)

    for c in loads:
        c.wait()
    for c in swaps:
        c.wait_recv()

    def delta_of(n, _):
        cols = tile(n * HEAD, HEAD)
        product = o[:, cols].astype(F32) * g[:, cols].astype(F32)
        delta[n] = jnp.sum(product.T, axis=0, keepdims=True)
        return 0

    lax.fori_loop(0, GROUP * HEADS, delta_of, 0)

    forward(2)
    start_near(3)
    gathered(1)
    send_tail(1)

    def step(j, _):
        for c in tail_copies(j):
            c.wait_recv()
        keys_t[...] = kv[j, :, :HEAD].T
        for a in range(GROUP):
            n = j * GROUP + a
            cols = tile(n * HEAD, HEAD)
            lanes = slice(a * CHIP_ROWS, (a + 1) * CHIP_ROWS)
            u = a % 2
            query = q[:, cols]
            top = None
            for t in range(KEYS // PART):
                r = slice(t * PART, (t + 1) * PART)
                part = dot(kv[j, r, :HEAD], query, NT) + bias[r, :]
                scores[u, r, :] = part
                part = jnp.max(part.reshape(PART // 8, 8, CHIP_ROWS), axis=0)
                top = part if top is None else jnp.maximum(top, part)
            top = jnp.max(top, axis=0, keepdims=True)
            total = None
            for t in range(KEYS // PART):
                r = slice(t * PART, (t + 1) * PART)
                part = jnp.exp2((scores[u, r, :] - top) * EXP_SCALE)
                scores[u, r, :] = part
                part = jnp.sum(part.reshape(PART // 8, 8, CHIP_ROWS), axis=0)
                total = part if total is None else total + part
            share = 1.0 / jnp.sum(total, axis=0, keepdims=True)
            grad = g[:, cols]
            shift = delta[n]
            for t in range(KEYS // PART):
                r = slice(t * PART, (t + 1) * PART)
                p = scores[u, r, :] * share
                probs[r, lanes] = p.astype(BF16)
                dp = dot(kv[j, r, HEAD:], grad, NT)
                dscore[r, lanes] = (p * (dp - shift)).astype(BF16)
        wide_q = tile(j * GROUP * HEAD, GROUP * HEAD)
        qs = q[:, wide_q]
        gs = g[:, wide_q]
        rows_q = jnp.concatenate([qs[:, i * HEAD : (i + 1) * HEAD] for i in range(GROUP)], axis=0)
        rows_g = jnp.concatenate([gs[:, i * HEAD : (i + 1) * HEAD] for i in range(GROUP)], axis=0)
        back_send[j, 0] = (dot(dscore[BLOCK:, :], rows_q) * SCALE).astype(BF16)
        back_send[j, 1] = dot(probs[BLOCK:, :], rows_g).astype(BF16)
        for c in back_copies(j):
            c.start()
        acc[j, :, :HEAD] = dot(dscore[:BLOCK, :], rows_q) * SCALE
        acc[j, :, HEAD:] = dot(probs[:BLOCK, :], rows_g)
        dq_t = dot(keys_t[...], dscore[...])
        for a in range(GROUP):
            dq[j, :, a * HEAD : (a + 1) * HEAD] = (dq_t[:, a * CHIP_ROWS : (a + 1) * CHIP_ROWS].T * SCALE).astype(BF16)
        for c in dq_copies(j):
            c.start()

        @pl.when(j == 0)
        def _():
            forward(3)

        @pl.when(j + eager >= 1)
        def _():
            hops_first(j - 1 + eager)

        @pl.when(j <= 1)
        def _():
            gathered(j + 2)
            send_tail(j + 2)

        @pl.when(j + eager >= 2)
        def _():
            hops_second(j - 2 + eager)

        return 0

    lax.fori_loop(0, HEADS, step, 0)
    hops_last(0)

    @pl.when(eager == 0)
    def _():
        hops_first(3)
        hops_second(2)

    hops_last(1)
    hops_last(2)
    hops_second(3)
    hops_last(3)

    for c in swaps:
        c.wait_send()

    def finish(j, _):
        for c in first_copies(j) + sib_copies(j):
            c.wait_send()
        for c in fwd_copies(j):
            c.wait_send()
        for c in tail_copies(j) + back_copies(j):
            c.wait_send()
        for n in range(6):
            hop(j, n).wait_send()
        own, other = dq_copies(j)
        own.wait()
        other.wait()
        own, other = kv_copies(j)
        for c in own + other:
            c.wait()
        return 0

    lax.fori_loop(0, HEADS, finish, 0)


def settle(a, b, c, x, y, z, sem):
    copies = [pltpu.make_async_copy(s, d, sem.at[i]) for i, (s, d) in enumerate(((a, x), (b, y), (c, z)))]
    for copy in copies:
        copy.start()
    for copy in copies:
        copy.wait()


def body(queries, keys, values, output, gradient, order):
    any_spec = pl.BlockSpec(memory_space=pl.ANY)
    wide = GROUP * HEADS * HEAD
    dma = pltpu.SemaphoreType.DMA
    grads = pl.pallas_call(
        kernel,
        out_shape=(
            jax.ShapeDtypeStruct(queries.shape, BF16),
            jax.ShapeDtypeStruct(keys.shape, BF16),
            jax.ShapeDtypeStruct(values.shape, BF16),
        ),
        in_specs=[any_spec] * 5 + [pl.BlockSpec(memory_space=pltpu.VMEM)],
        out_specs=[any_spec] * 3,
        scratch_shapes=[
            pltpu.VMEM((CHIP_ROWS, wide), BF16),
            pltpu.VMEM((CHIP_ROWS, wide), BF16),
            pltpu.VMEM((CHIP_ROWS, wide), BF16),
            pltpu.VMEM((HEADS, KEYS, 2 * HEAD), BF16),
            pltpu.VMEM((KEYS, CHIP_ROWS), F32),
            pltpu.VMEM((TAIL, BLOCK), BF16),
            pltpu.VMEM((BLOCK, TAIL), BF16),
            pltpu.VMEM((GROUP * HEADS, 1, CHIP_ROWS), F32),
            pltpu.VMEM((2, KEYS, CHIP_ROWS), F32),
            pltpu.VMEM((HEAD, KEYS), BF16),
            pltpu.VMEM((KEYS, GROUP * CHIP_ROWS), BF16),
            pltpu.VMEM((KEYS, GROUP * CHIP_ROWS), BF16),
            pltpu.VMEM((HEADS, BLOCK, 2 * HEAD), F32),
            pltpu.VMEM((HEADS, CHIP_ROWS, GROUP * HEAD), BF16),
            pltpu.VMEM((HEADS, 2, TAIL, HEAD), BF16),
            pltpu.VMEM((HEADS, 2, TAIL, HEAD), BF16),
            pltpu.VMEM((HEADS, 2, TAIL, HEAD), BF16),
            pltpu.VMEM((HEADS, 6, CHIP_ROWS, HEAD), BF16),
            pltpu.VMEM((HEADS, 6, CHIP_ROWS, HEAD), BF16),
            pltpu.VMEM((HEADS, CHIP_ROWS, 2 * HEAD), BF16),
            dma((3,)), dma((HEADS, 2)), dma((3,)), dma((3,)),
            dma((HEADS, 8)), dma((HEADS, 4)), dma((HEADS, 2)), dma((HEADS,)), dma((HEADS, 2)), dma((HEADS, 2)),
            dma((HEADS, 2)), dma((HEADS, 2)), dma((HEADS, 2)), dma((HEADS, 2)), dma((HEADS, 6)), dma((HEADS, 6)),
            dma((HEADS,)), dma((HEADS,)), dma((HEADS,)), dma((HEADS, 2)), dma((HEADS, 2)), dma((HEADS, 2)),
        ],
        compiler_params=pltpu.CompilerParams(
            collective_id=0, has_side_effects=True, vmem_limit_bytes=62 * 2**20
        ),
        name="banded_attention_grad",
    )(queries, keys, values, output, gradient, order)
    return pl.pallas_call(
        settle,
        out_shape=tuple(jax.ShapeDtypeStruct(x.shape, BF16) for x in grads),
        in_specs=[pl.BlockSpec(memory_space=pltpu.VMEM)] * 3,
        out_specs=[any_spec] * 3,
        scratch_shapes=[dma((3,))],
        name="settle",
    )(*grads)


def solution(mesh):
    spec = P(("ctx", "head"), None)
    return jax.shard_map(
        body,
        mesh=mesh,
        in_specs=(spec,) * 5 + (P("ctx", None),),
        out_specs=(spec,) * 3,
        check_vma=False,
    )
```

```python
import math

import jax
import jax.numpy as jnp
from jax import lax
from jax.experimental import pallas as pl
from jax.experimental.pallas import tpu as pltpu
from jax.sharding import PartitionSpec as P

HEAD = 128
HEADS = 4
GROUP = 4
ROWS = 128
CHIP_ROWS = 256
BLOCK = 1024
TAIL = 256
KEYS = BLOCK + TAIL
PART = 256
SCALE = 1.0 / math.sqrt(HEAD)
EXP_SCALE = SCALE * math.log2(math.e)
MASKED = -1e30
MESH = pl.DeviceIdType.MESH
F32 = jnp.float32
BF16 = jnp.bfloat16
NN = (((1,), (0,)), ((), ()))
NT = (((1,), (1,)), ((), ()))
TN = (((0,), (0,)), ((), ()))


def dot(a, b, dims=NN):
    return lax.dot_general(a, b, dims, preferred_element_type=F32)


def tile(start, size):
    return pl.ds(pl.multiple_of(start, size), size)


def kernel(
    q_in, k_in, v_in, o_in, g_in, order,
    dq_out, dk_out, dv_out,
    q, g, o, kv, bias, take, give, delta, scores, keys_t, probs, dscore, acc, dq,
    tail_send, back_send, back_recv, hop_send, hop_recv, out_stage,
    load_sem, own_sem, pair_send, pair_recv,
    first_send, first_recv, sib_send, sib_recv, fwd_send, fwd_recv,
    tail_ssem, tail_rsem, back_ssem, back_rsem, hop_ssem, hop_rsem,
    dq_own, dq_ssem, dq_rsem, kv_own, kv_ssem, kv_rsem,
):
    h = lax.axis_index("head")
    block = lax.axis_index("ctx")
    core = h % 2
    chip = h // 2
    right, left, far = (chip + 1) % 4, (chip + 3) % 4, (chip + 2) % 4
    sib = chip * 2 + 1 - core
    after, before = (block + 1) % 64, (block + 63) % 64
    bend_after = (block % 8 + 1) // 8 * (block // 8 % 2 * 2 - 1)
    bend_before = (before % 8 + 1) // 8 * (before // 8 % 2 * 2 - 1)
    eager = 1 - (block % 8 + 7) // 8
    lo, hi = pl.ds(0, HEAD), pl.ds(HEAD, HEAD)
    right_dev, left_dev, sib_dev = {"head": right * 2 + core}, {"head": left * 2 + core}, {"head": sib}

    def after_dev(n):
        return {"head": (chip + 4 + n * bend_after) % 4 * 2 + core, "ctx": after}

    def before_dev(n):
        return {"head": (chip + 4 - n * bend_before) % 4 * 2 + core, "ctx": before}

    own_rows = tile(core * ROWS, ROWS)
    sib_rows = tile((1 - core) * ROWS, ROWS)
    wide = GROUP * HEADS * HEAD
    own_cols = tile(core * wide, wide)
    sib_cols = tile((1 - core) * wide, wide)

    def remote(src, dst, ssem, rsem, dev):
        return pltpu.make_async_remote_copy(
            src_ref=src, dst_ref=dst, send_sem=ssem, recv_sem=rsem, device_id=dev, device_id_type=MESH
        )

    def landed(ref, sem):
        pltpu.make_async_copy(ref, ref, sem).wait()

    def chip_rows(c):
        return tile(c * CHIP_ROWS, CHIP_ROWS)

    def block_rows(c, k):
        return tile((c * 2 + k) * ROWS, ROWS)

    def head_cols(k, j):
        return tile((k * HEADS + j) * HEAD, HEAD)

    pairs = ((q_in, q), (g_in, g), (o_in, o))
    loads = [
        pltpu.make_async_copy(src.at[:, own_cols], dst.at[own_rows, :], load_sem.at[i])
        for i, (src, dst) in enumerate(pairs)
    ]
    for c in loads:
        c.start()

    barrier = pltpu.get_barrier_semaphore()
    for dev in (
        {"head": right * 2}, {"head": right * 2 + 1}, {"head": left * 2}, {"head": left * 2 + 1},
        sib_dev, before_dev(0), before_dev(1),
    ):
        pl.semaphore_signal(barrier, inc=1, device_id=dev, device_id_type=MESH)
    pl.semaphore_wait(barrier, 7)

    def first_copies(j, which=(0, 1, 2, 3)):
        kinds = ((k_in, lo, right), (v_in, hi, left), (k_in, lo, left), (v_in, hi, right))
        out = []
        for n in which:
            src, part, to = kinds[n]
            for k in range(2):
                out.append(
                    remote(
                        src.at[:, head_cols(k, j)], kv.at[j, block_rows(chip, core), part],
                        first_send.at[j, 2 * n + k], first_recv.at[j, n], {"head": to * 2 + k},
                    )
                )
        return out

    def sib_copies(j):
        return [
            remote(
                src.at[:, head_cols(1 - core, j)], kv.at[j, block_rows(chip, core), part],
                sib_send.at[j, n], sib_recv.at[j], sib_dev,
            )
            for n, (src, part) in enumerate(((k_in, lo), (v_in, hi)))
        ]

    def own_copies(j):
        return [
            pltpu.make_async_copy(
                src.at[:, head_cols(core, j)], kv.at[j, block_rows(chip, core), part], own_sem.at[j, n]
            )
            for n, (src, part) in enumerate(((k_in, lo), (v_in, hi)))
        ]

    def start_onward(j):
        for c in first_copies(j, (0, 1)) + sib_copies(j) + own_copies(j):
            c.start()

    def start_near(j):
        for c in first_copies(j, (2, 3)):
            c.start()

    def fwd_copies(j):
        return (
            remote(kv.at[j, chip_rows(left), lo], kv.at[j, chip_rows(left), lo],
                   fwd_send.at[j, 0], fwd_recv.at[j, 0], right_dev),
            remote(kv.at[j, chip_rows(right), hi], kv.at[j, chip_rows(right), hi],
                   fwd_send.at[j, 1], fwd_recv.at[j, 1], left_dev),
        )

    def forward(j):
        a, b = fwd_copies(j)
        landed(kv.at[j, chip_rows(left), lo], first_recv.at[j, 0])
        a.start()
        landed(kv.at[j, chip_rows(right), hi], first_recv.at[j, 1])
        b.start()

    def gathered(j):
        for c in own_copies(j):
            c.wait()
        landed(kv.at[j, block_rows(chip, 1 - core), :], sib_recv.at[j])
        landed(kv.at[j, chip_rows(right), lo], first_recv.at[j, 2])
        landed(kv.at[j, chip_rows(left), hi], first_recv.at[j, 3])
        landed(kv.at[j, chip_rows(far), lo], fwd_recv.at[j, 0])
        landed(kv.at[j, chip_rows(far), hi], fwd_recv.at[j, 1])

    halves = (slice(0, HEAD), slice(HEAD, 2 * HEAD))

    def tail_copies(j):
        return [
            remote(tail_send.at[j, n], kv.at[j, pl.ds(BLOCK, TAIL), part],
                   tail_ssem.at[j, n], tail_rsem.at[j, n], after_dev(n))
            for n, part in enumerate((lo, hi))
        ]

    def send_tail(j):
        rows = dot(take[...], kv[j, :BLOCK, :]).astype(BF16)
        for n, c in enumerate(tail_copies(j)):
            tail_send[j, n] = rows[:, halves[n]]
            c.start()

    def back_copies(j):
        return [
            remote(back_send.at[j, n], back_recv.at[j, n], back_ssem.at[j, n], back_rsem.at[j, n], before_dev(n))
            for n in range(2)
        ]

    def hop(j, n):
        dev = right_dev if n in (0, 3, 4) else left_dev
        return remote(hop_send.at[j, n], hop_recv.at[j, n], hop_ssem.at[j, n], hop_rsem.at[j, n], dev)

    def send_hop(j, n, value):
        hop_send[j, n] = value.astype(BF16)
        hop(j, n).start()

    def take_hop(j, n):
        hop(j, n).wait_recv()
        return hop_recv[j, n].astype(F32)

    def hops_first(j):
        for c in back_copies(j):
            c.wait_recv()
        back = jnp.concatenate([back_recv[j, 0], back_recv[j, 1]], axis=1)

        def whole(c):
            return acc[j, chip_rows(c), :] + dot(give[chip_rows(c), :], back)

        part = whole(far)
        send_hop(j, 0, part[:, :HEAD])
        send_hop(j, 1, part[:, HEAD:])
        part = whole(left)
        send_hop(j, 2, part[:, :HEAD])
        acc[j, chip_rows(left), HEAD:] = part[:, HEAD:]
        part = whole(right)
        send_hop(j, 3, part[:, HEAD:])
        acc[j, chip_rows(right), :HEAD] = part[:, :HEAD]
        acc[j, chip_rows(chip), :] = whole(chip)

    def hops_second(j):
        s = j
        send_hop(j, 4, acc[s, chip_rows(right), :HEAD] + take_hop(j, 0))
        send_hop(j, 5, acc[s, chip_rows(left), HEAD:] + take_hop(j, 1))

    def kv_copies(j):
        own, other = [], []
        for n, (dst, part) in enumerate(((dk_out, lo), (dv_out, hi))):
            cols = head_cols(core, j)
            own.append(pltpu.make_async_copy(out_stage.at[j, own_rows, part], dst.at[:, cols], kv_own.at[j, n]))
            other.append(
                remote(out_stage.at[j, sib_rows, part], dst.at[:, cols], kv_ssem.at[j, n], kv_rsem.at[j, n], sib_dev)
            )
        return own, other

    def hops_last(j):
        s = j
        out_stage[j, :, :HEAD] = (acc[s, chip_rows(chip), :HEAD] + take_hop(j, 2) + take_hop(j, 4)).astype(BF16)
        out_stage[j, :, HEAD:] = (acc[s, chip_rows(chip), HEAD:] + take_hop(j, 3) + take_hop(j, 5)).astype(BF16)
        own, other = kv_copies(j)
        for c in own + other:
            c.start()

    def dq_copies(j):
        cols = tile((core * HEADS + j) * GROUP * HEAD, GROUP * HEAD)
        return (
            pltpu.make_async_copy(dq.at[j, own_rows, :], dq_out.at[:, cols], dq_own.at[j]),
            remote(dq.at[j, sib_rows, :], dq_out.at[:, cols], dq_ssem.at[j], dq_rsem.at[j], sib_dev),
        )

    start_onward(0)
    start_near(0)
    swaps = [
        remote(src.at[:, sib_cols], dst.at[own_rows, :], pair_send.at[i], pair_recv.at[i], sib_dev)
        for i, (src, dst) in enumerate(pairs)
    ]
    for c in swaps:
        c.start()
    start_onward(1)

    order_f = order[...].astype(F32)
    place = lax.broadcasted_iota(jnp.int32, (TAIL, BLOCK), 0).astype(F32)
    take[...] = jnp.where(order_f == place + float(BLOCK - TAIL), 1.0, 0.0).astype(BF16)

    forward(0)
    start_near(1)
    start_onward(2)

    column = jnp.broadcast_to(order_f, (HEAD, BLOCK)).T
    mine = order[:, chip_rows(chip)].astype(F32)
    lane = lax.broadcasted_iota(jnp.int32, (BLOCK, HEAD), 1).astype(F32)
    for half in range(2):
        cols = slice(half * HEAD, (half + 1) * HEAD)
        bias[:BLOCK, cols] = jnp.where(column <= mine[:, cols], 0.0, MASKED)
        give[:, cols] = jnp.where(column == lane + float(BLOCK - TAIL + half * HEAD), 1.0, 0.0).astype(BF16)
    bias[BLOCK:, :] = jnp.full((TAIL, CHIP_ROWS), jnp.where(block > 0, 0.0, MASKED), F32)

    gathered(0)
    send_tail(0)
    forward(1)
    start_near(2)
    start_onward(3)

    for c in loads:
        c.wait()
    for c in swaps:
        c.wait_recv()

    def delta_of(n, _):
        cols = tile(n * HEAD, HEAD)
        product = o[:, cols].astype(F32) * g[:, cols].astype(F32)
        delta[n] = jnp.sum(product.T, axis=0, keepdims=True)
        return 0

    lax.fori_loop(0, GROUP * HEADS, delta_of, 0)

    forward(2)
    start_near(3)
    gathered(1)
    send_tail(1)

    def step(j, _):
        for c in tail_copies(j):
            c.wait_recv()
        keys_t[...] = kv[j, :, :HEAD].T
        for a in range(GROUP):
            n = j * GROUP + a
            cols = tile(n * HEAD, HEAD)
            lanes = slice(a * CHIP_ROWS, (a + 1) * CHIP_ROWS)
            u = a % 2
            query = q[:, cols]
            top = None
            for t in range(KEYS // PART):
                r = slice(t * PART, (t + 1) * PART)
                part = dot(kv[j, r, :HEAD], query, NT) + bias[r, :]
                scores[u, r, :] = part
                part = jnp.max(part.reshape(PART // 8, 8, CHIP_ROWS), axis=0)
                top = part if top is None else jnp.maximum(top, part)
            top = jnp.max(top, axis=0, keepdims=True)
            total = None
            for t in range(KEYS // PART):
                r = slice(t * PART, (t + 1) * PART)
                part = jnp.exp2((scores[u, r, :] - top) * EXP_SCALE)
                scores[u, r, :] = part
                part = jnp.sum(part.reshape(PART // 8, 8, CHIP_ROWS), axis=0)
                total = part if total is None else total + part
            share = 1.0 / jnp.sum(total, axis=0, keepdims=True)
            grad = g[:, cols]
            shift = delta[n]
            for t in range(KEYS // PART):
                r = slice(t * PART, (t + 1) * PART)
                p = scores[u, r, :] * share
                probs[r, lanes] = p.astype(BF16)
                dp = dot(kv[j, r, HEAD:], grad, NT)
                dscore[r, lanes] = (p * (dp - shift)).astype(BF16)
        wide_q = tile(j * GROUP * HEAD, GROUP * HEAD)
        qs = q[:, wide_q]
        gs = g[:, wide_q]
        rows_q = jnp.concatenate([qs[:, i * HEAD : (i + 1) * HEAD] for i in range(GROUP)], axis=0)
        rows_g = jnp.concatenate([gs[:, i * HEAD : (i + 1) * HEAD] for i in range(GROUP)], axis=0)
        back_send[j, 0] = (dot(dscore[BLOCK:, :], rows_q) * SCALE).astype(BF16)
        back_send[j, 1] = dot(probs[BLOCK:, :], rows_g).astype(BF16)
        for c in back_copies(j):
            c.start()
        acc[j, :, :HEAD] = dot(dscore[:BLOCK, :], rows_q) * SCALE
        acc[j, :, HEAD:] = dot(probs[:BLOCK, :], rows_g)
        dq_t = dot(keys_t[...], dscore[...])
        for a in range(GROUP):
            dq[j, :, a * HEAD : (a + 1) * HEAD] = (dq_t[:, a * CHIP_ROWS : (a + 1) * CHIP_ROWS].T * SCALE).astype(BF16)
        for c in dq_copies(j):
            c.start()

        @pl.when(j == 0)
        def _():
            forward(3)

        @pl.when(j + eager >= 1)
        def _():
            hops_first(j - 1 + eager)

        @pl.when(j <= 1)
        def _():
            gathered(j + 2)
            send_tail(j + 2)

        @pl.when(j + eager >= 2)
        def _():
            hops_second(j - 2 + eager)

        return 0

    lax.fori_loop(0, HEADS, step, 0)

    @pl.when(eager == 0)
    def _():
        hops_first(3)
        hops_second(2)

    hops_last(0)
    hops_second(3)
    hops_last(1)
    hops_last(2)
    hops_last(3)

    for c in swaps:
        c.wait_send()

    def finish(j, _):
        for c in first_copies(j) + sib_copies(j):
            c.wait_send()
        for c in fwd_copies(j):
            c.wait_send()
        for c in tail_copies(j) + back_copies(j):
            c.wait_send()
        for n in range(6):
            hop(j, n).wait_send()
        own, other = dq_copies(j)
        own.wait()
        other.wait()
        own, other = kv_copies(j)
        for c in own + other:
            c.wait()
        return 0

    lax.fori_loop(0, HEADS, finish, 0)


def settle(a, b, c, x, y, z, wide, keys, values, in_sem, out_sem):
    pieces = []
    for src, held, dst in ((a, wide, x), (b, keys, y), (c, values, z)):
        step = min(src.shape[1], BLOCK)
        for at in range(0, src.shape[1], step):
            part = pl.ds(at, step)
            n = len(pieces)
            pieces.append(
                (
                    pltpu.make_async_copy(src.at[:, part], held.at[:, part], in_sem.at[n]),
                    pltpu.make_async_copy(held.at[:, part], dst.at[:, part], out_sem.at[n]),
                )
            )
    for come, _ in pieces:
        come.start()
    for come, go in pieces:
        come.wait()
        go.start()
    for _, go in pieces:
        go.wait()


def body(queries, keys, values, output, gradient, order):
    any_spec = pl.BlockSpec(memory_space=pl.ANY)
    wide = GROUP * HEADS * HEAD
    dma = pltpu.SemaphoreType.DMA
    grads = pl.pallas_call(
        kernel,
        out_shape=(
            jax.ShapeDtypeStruct(queries.shape, BF16),
            jax.ShapeDtypeStruct(keys.shape, BF16),
            jax.ShapeDtypeStruct(values.shape, BF16),
        ),
        in_specs=[any_spec] * 5 + [pl.BlockSpec(memory_space=pltpu.VMEM)],
        out_specs=[any_spec] * 3,
        scratch_shapes=[
            pltpu.VMEM((CHIP_ROWS, wide), BF16),
            pltpu.VMEM((CHIP_ROWS, wide), BF16),
            pltpu.VMEM((CHIP_ROWS, wide), BF16),
            pltpu.VMEM((HEADS, KEYS, 2 * HEAD), BF16),
            pltpu.VMEM((KEYS, CHIP_ROWS), F32),
            pltpu.VMEM((TAIL, BLOCK), BF16),
            pltpu.VMEM((BLOCK, TAIL), BF16),
            pltpu.VMEM((GROUP * HEADS, 1, CHIP_ROWS), F32),
            pltpu.VMEM((2, KEYS, CHIP_ROWS), F32),
            pltpu.VMEM((HEAD, KEYS), BF16),
            pltpu.VMEM((KEYS, GROUP * CHIP_ROWS), BF16),
            pltpu.VMEM((KEYS, GROUP * CHIP_ROWS), BF16),
            pltpu.VMEM((HEADS, BLOCK, 2 * HEAD), F32),
            pltpu.VMEM((HEADS, CHIP_ROWS, GROUP * HEAD), BF16),
            pltpu.VMEM((HEADS, 2, TAIL, HEAD), BF16),
            pltpu.VMEM((HEADS, 2, TAIL, HEAD), BF16),
            pltpu.VMEM((HEADS, 2, TAIL, HEAD), BF16),
            pltpu.VMEM((HEADS, 6, CHIP_ROWS, HEAD), BF16),
            pltpu.VMEM((HEADS, 6, CHIP_ROWS, HEAD), BF16),
            pltpu.VMEM((HEADS, CHIP_ROWS, 2 * HEAD), BF16),
            dma((3,)), dma((HEADS, 2)), dma((3,)), dma((3,)),
            dma((HEADS, 8)), dma((HEADS, 4)), dma((HEADS, 2)), dma((HEADS,)), dma((HEADS, 2)), dma((HEADS, 2)),
            dma((HEADS, 2)), dma((HEADS, 2)), dma((HEADS, 2)), dma((HEADS, 2)), dma((HEADS, 6)), dma((HEADS, 6)),
            dma((HEADS,)), dma((HEADS,)), dma((HEADS,)), dma((HEADS, 2)), dma((HEADS, 2)), dma((HEADS, 2)),
        ],
        compiler_params=pltpu.CompilerParams(
            collective_id=0, has_side_effects=True, vmem_limit_bytes=62 * 2**20
        ),
        name="banded_attention_grad",
    )(queries, keys, values, output, gradient, order)
    return pl.pallas_call(
        settle,
        out_shape=tuple(jax.ShapeDtypeStruct(x.shape, BF16) for x in grads),
        in_specs=[any_spec] * 3,
        out_specs=[any_spec] * 3,
        scratch_shapes=[pltpu.VMEM(x.shape, BF16) for x in grads] + [dma((6,)), dma((6,))],
        compiler_params=pltpu.CompilerParams(vmem_limit_bytes=62 * 2**20),
        name="settle",
    )(*grads)


def solution(mesh):
    spec = P(("ctx", "head"), None)
    return jax.shard_map(
        body,
        mesh=mesh,
        in_specs=(spec,) * 5 + (P("ctx", None),),
        out_specs=(spec,) * 3,
        check_vma=False,
    )
```

```python
import math

import jax
import jax.numpy as jnp
from jax import lax
from jax.experimental import pallas as pl
from jax.experimental.pallas import tpu as pltpu
from jax.sharding import PartitionSpec as P

HEAD = 128
HEADS = 4
GROUP = 4
ROWS = 128
CHIP_ROWS = 256
BLOCK = 1024
TAIL = 256
KEYS = BLOCK + TAIL
PART = 256
SCALE = 1.0 / math.sqrt(HEAD)
EXP_SCALE = SCALE * math.log2(math.e)
MASKED = -1e30
MESH = pl.DeviceIdType.MESH
F32 = jnp.float32
BF16 = jnp.bfloat16
NN = (((1,), (0,)), ((), ()))
NT = (((1,), (1,)), ((), ()))
TN = (((0,), (0,)), ((), ()))


def dot(a, b, dims=NN):
    return lax.dot_general(a, b, dims, preferred_element_type=F32)


def tile(start, size):
    return pl.ds(pl.multiple_of(start, size), size)


def kernel(
    q_in, k_in, v_in, o_in, g_in, order,
    dq_out, dk_out, dv_out,
    q, g, o, kv, bias, take, give, delta, scores, keys_t, probs, dscore, acc, dq,
    tail_send, back_send, back_recv, hop_send, hop_recv, out_stage,
    load_sem, own_sem, pair_send, pair_recv,
    first_send, first_recv, sib_send, sib_recv, fwd_send, fwd_recv,
    tail_ssem, tail_rsem, back_ssem, back_rsem, hop_ssem, hop_rsem,
    dq_own, dq_ssem, dq_rsem, kv_own, kv_ssem, kv_rsem,
):
    h = lax.axis_index("head")
    block = lax.axis_index("ctx")
    core = h % 2
    chip = h // 2
    right, left, far = (chip + 1) % 4, (chip + 3) % 4, (chip + 2) % 4
    sib = chip * 2 + 1 - core
    after, before = (block + 1) % 64, (block + 63) % 64
    bend_after = (block % 8 + 1) // 8 * (block // 8 % 2 * 2 - 1)
    bend_before = (before % 8 + 1) // 8 * (before // 8 % 2 * 2 - 1)
    eager = 1 - (block % 8 + 7) // 8
    lo, hi = pl.ds(0, HEAD), pl.ds(HEAD, HEAD)
    right_dev, left_dev, sib_dev = {"head": right * 2 + core}, {"head": left * 2 + core}, {"head": sib}

    def after_dev(n):
        return {"head": (chip + 4 + n * bend_after) % 4 * 2 + core, "ctx": after}

    def before_dev(n):
        return {"head": (chip + 4 - n * bend_before) % 4 * 2 + core, "ctx": before}

    own_rows = tile(core * ROWS, ROWS)
    sib_rows = tile((1 - core) * ROWS, ROWS)
    wide = GROUP * HEADS * HEAD
    own_cols = tile(core * wide, wide)
    sib_cols = tile((1 - core) * wide, wide)

    def remote(src, dst, ssem, rsem, dev):
        return pltpu.make_async_remote_copy(
            src_ref=src, dst_ref=dst, send_sem=ssem, recv_sem=rsem, device_id=dev, device_id_type=MESH
        )

    def landed(ref, sem):
        pltpu.make_async_copy(ref, ref, sem).wait()

    def chip_rows(c):
        return tile(c * CHIP_ROWS, CHIP_ROWS)

    def block_rows(c, k):
        return tile((c * 2 + k) * ROWS, ROWS)

    def head_cols(k, j):
        return tile((k * HEADS + j) * HEAD, HEAD)

    pairs = ((q_in, q), (g_in, g), (o_in, o))
    loads = [
        pltpu.make_async_copy(src.at[:, own_cols], dst.at[own_rows, :], load_sem.at[i])
        for i, (src, dst) in enumerate(pairs)
    ]
    for c in loads:
        c.start()

    barrier = pltpu.get_barrier_semaphore()
    for dev in (
        {"head": right * 2}, {"head": right * 2 + 1}, {"head": left * 2}, {"head": left * 2 + 1},
        sib_dev, before_dev(0), before_dev(1),
    ):
        pl.semaphore_signal(barrier, inc=1, device_id=dev, device_id_type=MESH)
    pl.semaphore_wait(barrier, 7)

    def first_copies(j, which=(0, 1, 2, 3)):
        kinds = ((k_in, lo, right), (v_in, hi, left), (k_in, lo, left), (v_in, hi, right))
        out = []
        for n in which:
            src, part, to = kinds[n]
            for k in range(2):
                out.append(
                    remote(
                        src.at[:, head_cols(k, j)], kv.at[j, block_rows(chip, core), part],
                        first_send.at[j, 2 * n + k], first_recv.at[j, n], {"head": to * 2 + k},
                    )
                )
        return out

    def sib_copies(j):
        return [
            remote(
                src.at[:, head_cols(1 - core, j)], kv.at[j, block_rows(chip, core), part],
                sib_send.at[j, n], sib_recv.at[j], sib_dev,
            )
            for n, (src, part) in enumerate(((k_in, lo), (v_in, hi)))
        ]

    def own_copies(j):
        return [
            pltpu.make_async_copy(
                src.at[:, head_cols(core, j)], kv.at[j, block_rows(chip, core), part], own_sem.at[j, n]
            )
            for n, (src, part) in enumerate(((k_in, lo), (v_in, hi)))
        ]

    def start_onward(j):
        for c in first_copies(j, (0, 1)) + sib_copies(j) + own_copies(j):
            c.start()

    def start_near(j):
        for c in first_copies(j, (2, 3)):
            c.start()

    def fwd_copies(j):
        return (
            remote(kv.at[j, chip_rows(left), lo], kv.at[j, chip_rows(left), lo],
                   fwd_send.at[j, 0], fwd_recv.at[j, 0], right_dev),
            remote(kv.at[j, chip_rows(right), hi], kv.at[j, chip_rows(right), hi],
                   fwd_send.at[j, 1], fwd_recv.at[j, 1], left_dev),
        )

    def forward(j):
        a, b = fwd_copies(j)
        landed(kv.at[j, chip_rows(left), lo], first_recv.at[j, 0])
        a.start()
        landed(kv.at[j, chip_rows(right), hi], first_recv.at[j, 1])
        b.start()

    def gathered(j):
        for c in own_copies(j):
            c.wait()
        landed(kv.at[j, block_rows(chip, 1 - core), :], sib_recv.at[j])
        landed(kv.at[j, chip_rows(right), lo], first_recv.at[j, 2])
        landed(kv.at[j, chip_rows(left), hi], first_recv.at[j, 3])
        landed(kv.at[j, chip_rows(far), lo], fwd_recv.at[j, 0])
        landed(kv.at[j, chip_rows(far), hi], fwd_recv.at[j, 1])

    halves = (slice(0, HEAD), slice(HEAD, 2 * HEAD))

    def tail_copies(j):
        return [
            remote(tail_send.at[j, n], kv.at[j, pl.ds(BLOCK, TAIL), part],
                   tail_ssem.at[j, n], tail_rsem.at[j, n], after_dev(n))
            for n, part in enumerate((lo, hi))
        ]

    def send_tail(j):
        rows = dot(take[...], kv[j, :BLOCK, :]).astype(BF16)
        for n, c in enumerate(tail_copies(j)):
            tail_send[j, n] = rows[:, halves[n]]
            c.start()

    def back_copies(j):
        return [
            remote(back_send.at[j, n], back_recv.at[j, n], back_ssem.at[j, n], back_rsem.at[j, n], before_dev(n))
            for n in range(2)
        ]

    def hop(j, n):
        dev = right_dev if n in (0, 3, 4) else left_dev
        return remote(hop_send.at[j, n], hop_recv.at[j, n], hop_ssem.at[j, n], hop_rsem.at[j, n], dev)

    def send_hop(j, n, value):
        hop_send[j, n] = value.astype(BF16)
        hop(j, n).start()

    def take_hop(j, n):
        hop(j, n).wait_recv()
        return hop_recv[j, n].astype(F32)

    def hops_first(j):
        for c in back_copies(j):
            c.wait_recv()
        back = jnp.concatenate([back_recv[j, 0], back_recv[j, 1]], axis=1)

        def whole(c):
            return acc[j, chip_rows(c), :] + dot(give[chip_rows(c), :], back)

        part = whole(far)
        send_hop(j, 0, part[:, :HEAD])
        send_hop(j, 1, part[:, HEAD:])
        part = whole(left)
        send_hop(j, 2, part[:, :HEAD])
        acc[j, chip_rows(left), HEAD:] = part[:, HEAD:]
        part = whole(right)
        send_hop(j, 3, part[:, HEAD:])
        acc[j, chip_rows(right), :HEAD] = part[:, :HEAD]
        acc[j, chip_rows(chip), :] = whole(chip)

    def hops_second(j):
        s = j
        send_hop(j, 4, acc[s, chip_rows(right), :HEAD] + take_hop(j, 0))
        send_hop(j, 5, acc[s, chip_rows(left), HEAD:] + take_hop(j, 1))

    def kv_copies(j):
        own, other = [], []
        for n, (dst, part) in enumerate(((dk_out, lo), (dv_out, hi))):
            cols = head_cols(core, j)
            own.append(pltpu.make_async_copy(out_stage.at[j, own_rows, part], dst.at[:, cols], kv_own.at[j, n]))
            other.append(
                remote(out_stage.at[j, sib_rows, part], dst.at[:, cols], kv_ssem.at[j, n], kv_rsem.at[j, n], sib_dev)
            )
        return own, other

    def hops_last(j):
        s = j
        own, other = kv_copies(j)
        for n, (near, sums) in enumerate(((2, 4), (3, 5))):
            value = acc[s, chip_rows(chip), halves[n]] + take_hop(j, near) + take_hop(j, sums)
            out_stage[j, :, halves[n]] = value.astype(BF16)
            other[n].start()
            own[n].start()

    def dq_copies(j):
        cols = tile((core * HEADS + j) * GROUP * HEAD, GROUP * HEAD)
        return (
            pltpu.make_async_copy(dq.at[j, own_rows, :], dq_out.at[:, cols], dq_own.at[j]),
            remote(dq.at[j, sib_rows, :], dq_out.at[:, cols], dq_ssem.at[j], dq_rsem.at[j], sib_dev),
        )

    start_onward(0)
    start_near(0)
    swaps = [
        remote(src.at[:, sib_cols], dst.at[own_rows, :], pair_send.at[i], pair_recv.at[i], sib_dev)
        for i, (src, dst) in enumerate(pairs)
    ]
    for c in swaps:
        c.start()
    start_onward(1)

    order_f = order[...].astype(F32)
    place = lax.broadcasted_iota(jnp.int32, (TAIL, BLOCK), 0).astype(F32)
    take[...] = jnp.where(order_f == place + float(BLOCK - TAIL), 1.0, 0.0).astype(BF16)

    forward(0)
    start_near(1)
    start_onward(2)

    column = jnp.broadcast_to(order_f, (HEAD, BLOCK)).T
    mine = order[:, chip_rows(chip)].astype(F32)
    lane = lax.broadcasted_iota(jnp.int32, (BLOCK, HEAD), 1).astype(F32)
    for half in range(2):
        cols = slice(half * HEAD, (half + 1) * HEAD)
        bias[:BLOCK, cols] = jnp.where(column <= mine[:, cols], 0.0, MASKED)
        give[:, cols] = jnp.where(column == lane + float(BLOCK - TAIL + half * HEAD), 1.0, 0.0).astype(BF16)
    bias[BLOCK:, :] = jnp.full((TAIL, CHIP_ROWS), jnp.where(block > 0, 0.0, MASKED), F32)

    gathered(0)
    send_tail(0)
    forward(1)
    start_near(2)
    start_onward(3)

    for c in loads:
        c.wait()
    for c in swaps:
        c.wait_recv()

    def delta_of(n, _):
        cols = tile(n * HEAD, HEAD)
        product = o[:, cols].astype(F32) * g[:, cols].astype(F32)
        delta[n] = jnp.sum(product.T, axis=0, keepdims=True)
        return 0

    lax.fori_loop(0, GROUP * HEADS, delta_of, 0)

    forward(2)
    start_near(3)
    gathered(1)
    send_tail(1)

    def step(j, _):
        for c in tail_copies(j):
            c.wait_recv()
        keys_t[...] = kv[j, :, :HEAD].T
        for a in range(GROUP):
            n = j * GROUP + a
            cols = tile(n * HEAD, HEAD)
            lanes = slice(a * CHIP_ROWS, (a + 1) * CHIP_ROWS)
            u = a % 2
            query = q[:, cols]
            top = None
            for t in range(KEYS // PART):
                r = slice(t * PART, (t + 1) * PART)
                part = dot(kv[j, r, :HEAD], query, NT) + bias[r, :]
                scores[u, r, :] = part
                part = jnp.max(part.reshape(PART // 8, 8, CHIP_ROWS), axis=0)
                top = part if top is None else jnp.maximum(top, part)
            top = jnp.max(top, axis=0, keepdims=True)
            total = None
            for t in range(KEYS // PART):
                r = slice(t * PART, (t + 1) * PART)
                part = jnp.exp2((scores[u, r, :] - top) * EXP_SCALE)
                scores[u, r, :] = part
                part = jnp.sum(part.reshape(PART // 8, 8, CHIP_ROWS), axis=0)
                total = part if total is None else total + part
            share = 1.0 / jnp.sum(total, axis=0, keepdims=True)
            grad = g[:, cols]
            shift = delta[n]
            for t in range(KEYS // PART):
                r = slice(t * PART, (t + 1) * PART)
                p = scores[u, r, :] * share
                probs[r, lanes] = p.astype(BF16)
                dp = dot(kv[j, r, HEAD:], grad, NT)
                dscore[r, lanes] = (p * (dp - shift)).astype(BF16)
        wide_q = tile(j * GROUP * HEAD, GROUP * HEAD)
        qs = q[:, wide_q]
        gs = g[:, wide_q]
        rows_q = jnp.concatenate([qs[:, i * HEAD : (i + 1) * HEAD] for i in range(GROUP)], axis=0)
        rows_g = jnp.concatenate([gs[:, i * HEAD : (i + 1) * HEAD] for i in range(GROUP)], axis=0)
        back_send[j, 0] = (dot(dscore[BLOCK:, :], rows_q) * SCALE).astype(BF16)
        back_send[j, 1] = dot(probs[BLOCK:, :], rows_g).astype(BF16)
        for c in back_copies(j):
            c.start()
        acc[j, :, :HEAD] = dot(dscore[:BLOCK, :], rows_q) * SCALE
        acc[j, :, HEAD:] = dot(probs[:BLOCK, :], rows_g)
        dq_t = dot(keys_t[...], dscore[...])
        for a in range(GROUP):
            dq[j, :, a * HEAD : (a + 1) * HEAD] = (dq_t[:, a * CHIP_ROWS : (a + 1) * CHIP_ROWS].T * SCALE).astype(BF16)
        for c in dq_copies(j):
            c.start()

        @pl.when(j == 0)
        def _():
            forward(3)

        @pl.when(j + eager >= 1)
        def _():
            hops_first(j - 1 + eager)

        @pl.when(j <= 1)
        def _():
            gathered(j + 2)
            send_tail(j + 2)

        @pl.when(j + eager >= 2)
        def _():
            hops_second(j - 2 + eager)

        return 0

    lax.fori_loop(0, HEADS, step, 0)

    @pl.when(eager == 0)
    def _():
        hops_first(3)
        hops_second(2)

    hops_last(0)
    hops_second(3)
    hops_last(1)
    hops_last(2)
    hops_last(3)

    for c in swaps:
        c.wait_send()

    def finish(j, _):
        for c in first_copies(j) + sib_copies(j):
            c.wait_send()
        for c in fwd_copies(j):
            c.wait_send()
        for c in tail_copies(j) + back_copies(j):
            c.wait_send()
        for n in range(6):
            hop(j, n).wait_send()
        own, other = dq_copies(j)
        own.wait()
        other.wait()
        own, other = kv_copies(j)
        for c in own + other:
            c.wait()
        return 0

    lax.fori_loop(0, HEADS, finish, 0)


def settle(a, b, c, x, y, z, wide, keys, values, in_sem, out_sem):
    pieces = []
    for src, held, dst in ((a, wide, x), (b, keys, y), (c, values, z)):
        step = min(src.shape[1], BLOCK)
        for at in range(0, src.shape[1], step):
            part = pl.ds(at, step)
            n = len(pieces)
            pieces.append(
                (
                    pltpu.make_async_copy(src.at[:, part], held.at[:, part], in_sem.at[n]),
                    pltpu.make_async_copy(held.at[:, part], dst.at[:, part], out_sem.at[n]),
                )
            )
    for come, _ in pieces:
        come.start()
    for come, go in pieces:
        come.wait()
        go.start()
    for _, go in pieces:
        go.wait()


def body(queries, keys, values, output, gradient, order):
    any_spec = pl.BlockSpec(memory_space=pl.ANY)
    wide = GROUP * HEADS * HEAD
    dma = pltpu.SemaphoreType.DMA
    grads = pl.pallas_call(
        kernel,
        out_shape=(
            jax.ShapeDtypeStruct(queries.shape, BF16),
            jax.ShapeDtypeStruct(keys.shape, BF16),
            jax.ShapeDtypeStruct(values.shape, BF16),
        ),
        in_specs=[any_spec] * 5 + [pl.BlockSpec(memory_space=pltpu.VMEM)],
        out_specs=[any_spec] * 3,
        scratch_shapes=[
            pltpu.VMEM((CHIP_ROWS, wide), BF16),
            pltpu.VMEM((CHIP_ROWS, wide), BF16),
            pltpu.VMEM((CHIP_ROWS, wide), BF16),
            pltpu.VMEM((HEADS, KEYS, 2 * HEAD), BF16),
            pltpu.VMEM((KEYS, CHIP_ROWS), F32),
            pltpu.VMEM((TAIL, BLOCK), BF16),
            pltpu.VMEM((BLOCK, TAIL), BF16),
            pltpu.VMEM((GROUP * HEADS, 1, CHIP_ROWS), F32),
            pltpu.VMEM((2, KEYS, CHIP_ROWS), F32),
            pltpu.VMEM((HEAD, KEYS), BF16),
            pltpu.VMEM((KEYS, GROUP * CHIP_ROWS), BF16),
            pltpu.VMEM((KEYS, GROUP * CHIP_ROWS), BF16),
            pltpu.VMEM((HEADS, BLOCK, 2 * HEAD), F32),
            pltpu.VMEM((HEADS, CHIP_ROWS, GROUP * HEAD), BF16),
            pltpu.VMEM((HEADS, 2, TAIL, HEAD), BF16),
            pltpu.VMEM((HEADS, 2, TAIL, HEAD), BF16),
            pltpu.VMEM((HEADS, 2, TAIL, HEAD), BF16),
            pltpu.VMEM((HEADS, 6, CHIP_ROWS, HEAD), BF16),
            pltpu.VMEM((HEADS, 6, CHIP_ROWS, HEAD), BF16),
            pltpu.VMEM((HEADS, CHIP_ROWS, 2 * HEAD), BF16),
            dma((3,)), dma((HEADS, 2)), dma((3,)), dma((3,)),
            dma((HEADS, 8)), dma((HEADS, 4)), dma((HEADS, 2)), dma((HEADS,)), dma((HEADS, 2)), dma((HEADS, 2)),
            dma((HEADS, 2)), dma((HEADS, 2)), dma((HEADS, 2)), dma((HEADS, 2)), dma((HEADS, 6)), dma((HEADS, 6)),
            dma((HEADS,)), dma((HEADS,)), dma((HEADS,)), dma((HEADS, 2)), dma((HEADS, 2)), dma((HEADS, 2)),
        ],
        compiler_params=pltpu.CompilerParams(
            collective_id=0, has_side_effects=True, vmem_limit_bytes=62 * 2**20
        ),
        name="banded_attention_grad",
    )(queries, keys, values, output, gradient, order)
    return pl.pallas_call(
        settle,
        out_shape=tuple(jax.ShapeDtypeStruct(x.shape, BF16) for x in grads),
        in_specs=[any_spec] * 3,
        out_specs=[any_spec] * 3,
        scratch_shapes=[pltpu.VMEM(x.shape, BF16) for x in grads] + [dma((6,)), dma((6,))],
        compiler_params=pltpu.CompilerParams(vmem_limit_bytes=62 * 2**20),
        name="settle",
    )(*grads)


def solution(mesh):
    spec = P(("ctx", "head"), None)
    return jax.shard_map(
        body,
        mesh=mesh,
        in_specs=(spec,) * 5 + (P("ctx", None),),
        out_specs=(spec,) * 3,
        check_vma=False,
    )
```
